32 devices in a mesh: groups: 2 (over y), ctx: 4 (over z), head: 4 (over x, core).
Axes of the slice: x: 2, y: 2, z: 4, core: 2. Of those that a mesh axis runs over, the one named last changes fastest.
Arguments:
- queries: bfloat16 [32768, 2048], P(('groups', 'ctx'), 'head'), parts along dimension 0, may hold values from -6 to 6
- key_vectors: bfloat16 [32768, 2048], P(('groups', 'ctx'), 'head'), parts along dimension 0, may hold values from -0.52734375 to 0.52734375
- value_vectors: bfloat16 [32768, 2048], P(('groups', 'ctx'), 'head'), parts along dimension 0, may hold values from -6 to 6
- token_rows: int32 [32768], P(('groups', 'ctx')), parts along dimension 0, may hold values from 0 to 63
- weight_table: float32 [64, 16, 21], P(None, 'head'), may hold values from 0.1 to 1
Outputs:
- attended: bfloat16 [32768, 2048], P(('groups', 'ctx'), 'head'), parts along dimension 0
The draws below stay inside these ranges and needn't reach their ends.
There are 2 independent parts, one for each index of `groups`. The reference program is written for one: setup_inputs(seed, part) draws one part's arguments, and reference() takes and returns one part's arrays. A program takes and returns all parts, laid end to end along the dimension named above; an argument that names none is the same for every part. Nothing has to cross between parts.
All inputs are finite; a program needn't handle non-finite values.
Results may differ from the reference program's by a relative error of at most 0.004.
Values sent between devices are 32-bit elements; how exact they have to be, the bound alone decides.
A program may use at most 128 MiB of HBM per device.

```python
import math
import jax
import jax.numpy as jnp
from jax import lax

HEADS = 16
HEAD_DIM = 128
BLOCK = 256
LEVELS = 21
TABLE_ROWS = 64
TOKENS = 16384


def plant(result, stream_key, smallest, high):
    dims = result.shape
    index_at = [jax.random.randint(jax.random.fold_in(stream_key, axis), (), 0, dims[axis]) for axis in range(len(dims))]
    result = result.at[tuple(index_at)].set(smallest)
    longest = dims.index(max(dims))
    index_at[longest] = (index_at[longest] + 1) % dims[longest]
    return result.at[tuple(index_at)].set(high)


def steps_of(own_key, dims, pieces, low, high):
    level, own = 1.0, jax.random.fold_in(own_key, 6)
    for dim, shards_of in pieces:
        heights = jnp.exp(jax.random.uniform(jax.random.fold_in(own, dim), (shards_of,), jnp.float32, low / len(pieces), high / len(pieces)))
        level = level * jnp.repeat(heights, dims[dim] // shards_of).reshape([-1 if axis == dim else 1 for axis in range(len(dims))])
    return level


def scatter_about(stream_key, dims, scale, limit, split=(), kind=jnp.bfloat16):
    level = steps_of(stream_key, dims, split, -0.22, 0.18) if split else 1.0
    values = jax.random.normal(stream_key, dims, jnp.float32) * scale * level
    return jnp.minimum(jnp.maximum(values, -limit), limit).astype(kind)


def setup_inputs(seed: int = 0, part: int = 0) -> dict:
    streams_of = jax.random.split(jax.random.key(seed), 6)
    part_keys = jax.random.split(jax.random.fold_in(streams_of[5], part), 6)
    return {
        "queries": scatter_about(part_keys[0], (TOKENS, HEADS * HEAD_DIM), 1.0, 6.0, ((0, 4), (1, 4))),
        "key_vectors": scatter_about(part_keys[1], (TOKENS, HEADS * HEAD_DIM), (HEAD_DIM ** -0.5), 0.52734375, ((0, 4), (1, 4))),
        "value_vectors": scatter_about(part_keys[2], (TOKENS, HEADS * HEAD_DIM), 1.0, 6.0, ((0, 4), (1, 4))),
        "token_rows": plant(jax.random.randint(part_keys[3], (TOKENS,), 0, TABLE_ROWS), jax.random.fold_in(part_keys[3], 1), 0, TABLE_ROWS - 1).astype(jnp.int32),
        "weight_table": jnp.clip(jnp.exp(math.log(1.0) - 2.3025851 * jax.random.uniform(streams_of[4], (TABLE_ROWS, HEADS, LEVELS), jnp.float32) ** steps_of(streams_of[4], (TABLE_ROWS, HEADS, LEVELS), ((1, 4),), -0.2, 0.2)), 0.1, 1.0),
    }


def level_scale(level_count):
    level_ids = jnp.arange(level_count).astype(jnp.float32)
    return jnp.where(level_ids < 0.5, 1.0, 2.0 ** (-(level_ids - 1.0) / 2.0)).astype(jnp.float32)


def pair_levels(block_rows, block_bits):
    positions = jnp.arange(block_rows, dtype=jnp.int32)
    differing = jnp.bitwise_xor(positions[:, None], positions[None, :])
    pair_level = jnp.zeros((block_rows, block_rows), jnp.int32)
    for level_bit in range(block_bits):
        pair_level = pair_level + (differing >= 2 ** level_bit).astype(jnp.int32)
    pair_level = jnp.where(positions[None, :] <= positions[:, None], pair_level, -1)
    level_ids = jnp.arange(block_bits + 1, dtype=jnp.int32)
    return (pair_level[:, :, None] == level_ids[None, None, :]).astype(jnp.float32)


def reference(queries, key_vectors, value_vectors, token_rows, weight_table):
    token_count = queries.shape[0]
    block_rows = BLOCK
    block_count = token_count // block_rows
    block_bits = block_rows.bit_length() - 1
    all_bits = token_count.bit_length() - 1
    level_weight = weight_table[token_rows] * level_scale(LEVELS)[None, None, :]
    query_blocks = queries.astype(jnp.float32).reshape(block_count, block_rows, HEADS, HEAD_DIM)
    key_blocks = key_vectors.astype(jnp.float32).reshape(block_count, block_rows, HEADS, HEAD_DIM)
    value_blocks = value_vectors.astype(jnp.float32).reshape(block_count, block_rows, HEADS, HEAD_DIM)
    weight_blocks = level_weight.reshape(block_count, block_rows, HEADS, LEVELS)
    level_pick = pair_levels(block_rows, block_bits)

    def inside(block_index):
        query_one = query_blocks[block_index]
        key_one = key_blocks[block_index]
        value_one = value_blocks[block_index]
        weights_one = weight_blocks[block_index]
        pair_weight = jnp.einsum("thl,tsl->hts", weights_one[:, :, :block_bits + 1], level_pick,
                                 precision=lax.Precision.HIGHEST)
        scores = jnp.einsum("thd,shd->hts", query_one, key_one, precision=lax.Precision.HIGHEST)
        weighted = (scores * pair_weight).astype(jnp.bfloat16)
        weighted = lax.optimization_barrier(weighted).astype(jnp.float32)
        return jnp.einsum("hts,shd->thd", weighted, value_one, precision=lax.Precision.HIGHEST)

    result_sum = lax.map(inside, jnp.arange(block_count))
    block_states = jnp.einsum("bshd,bshe->bhde", key_blocks, value_blocks, precision=lax.Precision.HIGHEST)
    for level_bit in range(all_bits - block_bits):
        level_id = block_bits + 1 + level_bit
        span_blocks = 2 ** level_bit
        group_count = block_count // (2 * span_blocks)
        left_sum = block_states.reshape(group_count, 2, span_blocks, HEADS, HEAD_DIM, HEAD_DIM)[:, 0].sum(axis=1)
        right_query = query_blocks.reshape(group_count, 2, span_blocks * block_rows, HEADS, HEAD_DIM)[:, 1]
        product = jnp.einsum("gthd,ghde->gthe", right_query, left_sum, precision=lax.Precision.HIGHEST)
        right_weight = weight_blocks.reshape(group_count, 2, span_blocks * block_rows, HEADS, LEVELS)[:, 1, :, :, level_id]
        result_sum = result_sum.reshape(group_count, 2, span_blocks * block_rows, HEADS, HEAD_DIM)
        result_sum = result_sum.at[:, 1].add(right_weight[..., None] * product)
    return result_sum.reshape(token_count, HEADS * HEAD_DIM).astype(jnp.bfloat16)
```

```python
import functools

import jax
import jax.numpy as jnp
from jax import lax
from jax.experimental import pallas as pl
from jax.experimental.pallas import tpu as pltpu
from jax.sharding import PartitionSpec as P

BLOCK = 256
HALF = 128
WIDTH = 128
NT = (((1,), (1,)), ((), ()))


def level_constant(level_id):
    return 1.0 if level_id == 0 else 2.0 ** (-(level_id - 1) / 2.0)


def round_up(size, unit):
    return (size + unit - 1) // unit * unit


def node_index(block_count, bit, group):
    start = sum(block_count >> (low + 1) for low in range(bit))
    return start + group


def pair_tile(weight_rows):
    near_row = lax.broadcasted_iota(jnp.int32, (8, HALF), 0)
    near_lane = lax.broadcasted_iota(jnp.int32, (8, HALF), 1)
    near_target = near_lane & 7
    near_xor = near_row ^ near_target
    near = jnp.where(near_xor >= 1, weight_rows[1], weight_rows[0])
    near = jnp.where(near_xor >= 2, weight_rows[2], near)
    near = jnp.where(near_xor >= 4, weight_rows[3], near)
    near = jnp.where(near_row <= near_target, near, 0.0)
    far_row = lax.broadcasted_iota(jnp.int32, (16, HALF), 0)
    far_target = lax.broadcasted_iota(jnp.int32, (16, HALF), 1) >> 3
    far_xor = far_row ^ far_target
    far = jnp.where(far_xor >= 2, weight_rows[5], weight_rows[4])
    far = jnp.where(far_xor >= 4, weight_rows[6], far)
    far = jnp.where(far_xor >= 8, weight_rows[7], far)
    far = jnp.where(far_row <= far_target, far, 0.0)
    lane_group = near_lane >> 3
    return jnp.concatenate(
        [jnp.where(lane_group == row, near, far[row : row + 1]) for row in range(16)], axis=0
    )


def kernel(
    sizes,
    q_hbm,
    k_hbm,
    v_hbm,
    tok_ref,
    tab_ref,
    out_hbm,
    q_v,
    k_v,
    v_v,
    vt_v,
    out_v,
    acc,
    nodes,
    left,
    total,
    lift,
    remote,
    weights,
    table_pad,
    load_sem,
    out_sem,
    send_sem,
    recv_sem,
):
    head_count, block_count, level_count, table_count, shards, device_bits = sizes
    block_bits = BLOCK.bit_length() - 1
    local_bits = block_count.bit_length() - 1
    padded = round_up(level_count, 8)
    me = lax.axis_index("ctx")

    def load(array_id, head_id):
        source = (k_hbm, v_hbm, q_hbm)[array_id]
        target = (k_v, v_v, q_v)[array_id]
        column = pl.multiple_of(head_id * WIDTH, WIDTH)
        return pltpu.make_async_copy(
            source.at[:, pl.ds(column, WIDTH)], target.at[head_id], load_sem.at[array_id, head_id]
        )

    for head_id in range(head_count):
        load(0, head_id).start()
        load(1, head_id).start()
    for head_id in range(head_count):
        load(2, head_id).start()

    if shards > 1:
        barrier = pltpu.get_barrier_semaphore()

        @pl.when(me > 0)
        def _():
            pl.semaphore_signal(
                barrier, inc=1, device_id={"ctx": me - 1}, device_id_type=pl.DeviceIdType.MESH
            )

    level_row = lax.broadcasted_iota(jnp.int32, (padded, WIDTH), 0)
    scale = jnp.zeros((padded, WIDTH), jnp.float32)
    for level_id in range(level_count):
        scale = jnp.where(level_row == level_id, level_constant(level_id), scale)
    table_rows = []
    table_pad[...] = jnp.zeros_like(table_pad)
    for head_id in range(head_count):
        table_pad[0:table_count, 0:level_count] = tab_ref[:, head_id, :]
        table_rows.append(jnp.transpose(table_pad[...])[0:padded] * scale)
    table_all = jnp.concatenate(table_rows, axis=0)
    high = table_all.astype(jnp.bfloat16)
    rest = table_all - high.astype(jnp.float32)
    middle = rest.astype(jnp.bfloat16)
    low = (rest - middle.astype(jnp.float32)).astype(jnp.bfloat16)
    split = jnp.concatenate([high, middle, low], axis=0)
    rows = head_count * padded

    def weigh(block, carry):
        tokens = jnp.concatenate(
            [tok_ref[pl.ds(2 * block, 1), :], tok_ref[pl.ds(2 * block + 1, 1), :]], axis=1
        )
        picks = lax.broadcasted_iota(jnp.int32, (WIDTH, BLOCK), 0) == tokens
        one_hot = jnp.where(picks, 1.0, 0.0).astype(jnp.bfloat16)
        parts = jnp.dot(split, one_hot, preferred_element_type=jnp.float32)
        weights[block] = parts[0:rows] + parts[rows : 2 * rows] + parts[2 * rows :]
        return carry

    lax.fori_loop(0, block_count, weigh, 0)

    def remote_copy(source, bit, head_id):
        return pltpu.make_async_remote_copy(
            src_ref=source,
            dst_ref=remote.at[bit, head_id],
            send_sem=send_sem.at[bit, head_id],
            recv_sem=recv_sem.at[bit, head_id],
            device_id={"ctx": me + 1},
            device_id_type=pl.DeviceIdType.MESH,
        )

    def has_bit(bit):
        return lax.rem(lax.div(me, 2**bit), 2) == 1

    def ends_span(bit):
        return lax.rem(me, 2**bit) == 2**bit - 1

    def is_source(bit):
        return jnp.logical_and(ends_span(bit), jnp.logical_not(has_bit(bit)))

    def is_relay(bit):
        return jnp.logical_and(has_bit(bit), jnp.logical_not(ends_span(bit)))

    if shards > 1:

        @pl.when(me < shards - 1)
        def _():
            pl.semaphore_wait(barrier, 1)

    def states(head_id, carry):
        load(0, head_id).wait()
        load(1, head_id).wait()
        for block in range(block_count):
            span = pl.ds(block * BLOCK, BLOCK)
            value_t = jnp.transpose(v_v[head_id, span, :])
            vt_v[head_id, :, span] = value_t
            state = jnp.dot(value_t, k_v[head_id, span, :], preferred_element_type=jnp.float32)
            bit = 0
            while block >> bit & 1:
                state = left[bit] + state
                bit += 1
            if bit < local_bits:
                left[bit] = state
                nodes[head_id, node_index(block_count, bit, block >> (bit + 1))] = state.astype(
                    jnp.bfloat16
                )
            else:
                total[head_id] = state
        for bit in range(device_bits):

            @pl.when(jnp.logical_not(has_bit(bit)))
            def _(bit=bit):
                remote[bit, head_id] = jnp.zeros((WIDTH, WIDTH), jnp.float32)

        if shards > 1:

            @pl.when(is_source(0))
            def _():
                remote_copy(total.at[head_id], 0, head_id).start()

        return carry

    lax.fori_loop(0, head_count, states, 0)

    def service(bit, head_id):
        @pl.when(has_bit(bit))
        def _():
            remote_copy(total.at[head_id], bit, head_id).wait_recv()

        @pl.when(is_relay(bit))
        def _():
            remote_copy(remote.at[bit, head_id], bit, head_id).start()

        if bit + 1 < device_bits:

            @pl.when(ends_span(bit + 1))
            def _():
                base = total[head_id] if bit == 0 else lift[bit - 1, head_id]
                lift[bit, head_id] = base + remote[bit, head_id]

            @pl.when(is_source(bit + 1))
            def _():
                remote_copy(lift.at[bit, head_id], bit + 1, head_id).start()

    pace = 2 if head_count % 2 == 0 else 1
    steps = head_count // pace

    def weight_row(block, head_id, level_id):
        return weights[block, pl.ds(head_id * padded + level_id, 1), :]

    def inside(head_id, carry):
        load(2, head_id).wait()
        for block in range(block_count):
            if block % (block_count // pace) == 0:
                for bit in range(device_bits):
                    step = head_id - bit

                    @pl.when(jnp.logical_and(step >= 0, step < steps))
                    def _(bit=bit, step=step, block=block):
                        service(bit, step * pace + block // (block_count // pace))

            span = pl.ds(block * BLOCK, BLOCK)
            bits = [bit for bit in range(local_bits) if block >> bit & 1]
            stack = [k_v[head_id, span, :]] + [
                nodes[head_id, node_index(block_count, bit, block >> (bit + 1))] for bit in bits
            ]
            lines = jnp.concatenate(stack, axis=0)
            product = lax.dot_general(
                lines, q_v[head_id, span, :], NT, preferred_element_type=jnp.float32
            )
            level_rows = [
                weight_row(block, head_id, level_id) for level_id in range(block_bits + 1)
            ]
            first = pair_tile([row[:, :HALF] for row in level_rows])
            second = pair_tile([row[:, HALF:] for row in level_rows])
            top = jnp.concatenate(
                [
                    (product[:HALF, :HALF] * first).astype(jnp.bfloat16),
                    (product[:HALF, HALF:] * level_rows[block_bits][:, HALF:]).astype(jnp.bfloat16),
                ],
                axis=1,
            )
            bottom = jnp.concatenate(
                [
                    jnp.zeros((HALF, HALF), jnp.bfloat16),
                    (product[HALF:BLOCK, HALF:] * second).astype(jnp.bfloat16),
                ],
                axis=1,
            )
            weighted = jnp.concatenate([top, bottom], axis=0)
            result = jnp.dot(vt_v[head_id, :, span], weighted, preferred_element_type=jnp.float32)
            for place, bit in enumerate(bits):
                begin = BLOCK + place * WIDTH
                result = result + product[begin : begin + WIDTH] * weight_row(
                    block, head_id, block_bits + 1 + bit
                )
            acc[head_id, block] = result
        return carry

    lax.fori_loop(0, head_count, inside, 0)
    for late in range(head_count, steps + device_bits - 1):
        for bit in range(device_bits):
            step = late - bit
            if 0 <= step < steps:
                for place in range(pace):
                    service(bit, step * pace + place)

    chunk = max(1, block_count // 4)

    def write(head_id, part):
        column = pl.multiple_of(head_id * WIDTH, WIDTH)
        lines = pl.ds(part * chunk * BLOCK, chunk * BLOCK)
        return pltpu.make_async_copy(
            out_v.at[head_id, lines, :],
            out_hbm.at[lines, pl.ds(column, WIDTH)],
            out_sem.at[head_id, part],
        )

    def finish(head_id, carry):
        if device_bits:
            lines = jnp.concatenate(
                [remote[bit, head_id].astype(jnp.bfloat16) for bit in range(device_bits)], axis=0
            )
        for block in range(block_count):
            span = pl.ds(block * BLOCK, BLOCK)
            result = acc[head_id, block]
            if device_bits:
                product = lax.dot_general(
                    lines, q_v[head_id, span, :], NT, preferred_element_type=jnp.float32
                )
            for bit in range(device_bits):
                result = result + product[bit * WIDTH : (bit + 1) * WIDTH] * weight_row(
                    block, head_id, block_bits + local_bits + 1 + bit
                )
            out_v[head_id, span, :] = jnp.transpose(result.astype(jnp.bfloat16))
            if block % chunk == chunk - 1:
                write(head_id, block // chunk).start()
        return carry

    lax.fori_loop(0, head_count, finish, 0)
    for head_id in range(head_count):
        for part in range(block_count // chunk):
            write(head_id, part).wait()
    for bit in range(device_bits):

        @pl.when(jnp.logical_or(is_source(bit), is_relay(bit)))
        def _(bit=bit):
            for head_id in range(head_count):
                remote_copy(total.at[head_id], bit, head_id).wait_send()


def body(queries, key_vectors, value_vectors, token_rows, weight_table):
    table_count, head_count, level_count = weight_table.shape
    token_count = queries.shape[0]
    block_count = token_count // BLOCK
    shards = lax.axis_size("ctx")
    device_bits = shards.bit_length() - 1
    padded = round_up(level_count, 8)
    slots = max(1, device_bits)
    sizes = (head_count, block_count, level_count, table_count, shards, device_bits)
    hbm = pl.BlockSpec(memory_space=pl.ANY)
    vmem = pl.BlockSpec(memory_space=pltpu.VMEM)
    wide = (head_count, token_count, WIDTH)
    state = (WIDTH, WIDTH)
    return pl.pallas_call(
        functools.partial(kernel, sizes),
        out_shape=jax.ShapeDtypeStruct(queries.shape, jnp.bfloat16),
        in_specs=[hbm, hbm, hbm, vmem, vmem],
        out_specs=hbm,
        scratch_shapes=[
            pltpu.VMEM(wide, jnp.bfloat16),
            pltpu.VMEM(wide, jnp.bfloat16),
            pltpu.VMEM(wide, jnp.bfloat16),
            pltpu.VMEM((head_count, WIDTH, token_count), jnp.bfloat16),
            pltpu.VMEM(wide, jnp.bfloat16),
            pltpu.VMEM((head_count, block_count, WIDTH, BLOCK), jnp.float32),
            pltpu.VMEM((head_count, max(1, block_count - 1)) + state, jnp.bfloat16),
            pltpu.VMEM((max(1, block_count.bit_length() - 1),) + state, jnp.float32),
            pltpu.VMEM((head_count,) + state, jnp.float32),
            pltpu.VMEM((slots, head_count) + state, jnp.float32),
            pltpu.VMEM((slots, head_count) + state, jnp.float32),
            pltpu.VMEM((block_count, head_count * padded, BLOCK), jnp.float32),
            pltpu.VMEM((WIDTH, WIDTH), jnp.float32),
            pltpu.SemaphoreType.DMA((3, head_count)),
            pltpu.SemaphoreType.DMA((head_count, 4)),
            pltpu.SemaphoreType.DMA((slots, head_count)),
            pltpu.SemaphoreType.DMA((slots, head_count)),
        ],
        compiler_params=pltpu.CompilerParams(
            collective_id=0, has_side_effects=True, vmem_limit_bytes=48 * 1024 * 1024
        ),
        cost_estimate=pl.CostEstimate(
            flops=10 * token_count * head_count * WIDTH * BLOCK,
            bytes_accessed=8 * token_count * head_count * WIDTH,
            transcendentals=0,
        ),
    )(
        queries,
        key_vectors,
        value_vectors,
        token_rows.reshape(token_count // WIDTH, WIDTH),
        weight_table,
    )


def solution(mesh):
    placed = (
        P(("groups", "ctx"), "head"),
        P(("groups", "ctx"), "head"),
        P(("groups", "ctx"), "head"),
        P(("groups", "ctx")),
        P(None, "head", None),
    )
    return jax.shard_map(
        body, mesh=mesh, in_specs=placed, out_specs=P(("groups", "ctx"), "head"), check_vma=False
    )
```

```python
import functools

import jax
import jax.numpy as jnp
from jax import lax
from jax.experimental import pallas as pl
from jax.experimental.pallas import tpu as pltpu
from jax.sharding import PartitionSpec as P

BLOCK = 256
HALF = 128
WIDTH = 128
NT = (((1,), (1,)), ((), ()))


def level_constant(level_id):
    return 1.0 if level_id == 0 else 2.0 ** (-(level_id - 1) / 2.0)


def round_up(size, unit):
    return (size + unit - 1) // unit * unit


def node_index(block_count, bit, group):
    start = sum(block_count >> (low + 1) for low in range(bit))
    return start + group


def pair_tile(weight_rows):
    near_row = lax.broadcasted_iota(jnp.int32, (8, HALF), 0)
    near_lane = lax.broadcasted_iota(jnp.int32, (8, HALF), 1)
    near_target = near_lane & 7
    near_xor = near_row ^ near_target
    near = jnp.where(near_xor >= 1, weight_rows[1], weight_rows[0])
    near = jnp.where(near_xor >= 2, weight_rows[2], near)
    near = jnp.where(near_xor >= 4, weight_rows[3], near)
    near = jnp.where(near_row <= near_target, near, 0.0)
    far_row = lax.broadcasted_iota(jnp.int32, (16, HALF), 0)
    far_target = lax.broadcasted_iota(jnp.int32, (16, HALF), 1) >> 3
    far_xor = far_row ^ far_target
    far = jnp.where(far_xor >= 2, weight_rows[5], weight_rows[4])
    far = jnp.where(far_xor >= 4, weight_rows[6], far)
    far = jnp.where(far_xor >= 8, weight_rows[7], far)
    far = jnp.where(far_row <= far_target, far, 0.0)
    lane_group = near_lane >> 3
    return jnp.concatenate(
        [jnp.where(lane_group == row, near, far[row : row + 1]) for row in range(16)], axis=0
    )


def kernel(
    sizes,
    q_hbm,
    k_hbm,
    v_hbm,
    tok_hbm,
    tab_hbm,
    out_hbm,
    acc,
    q_v,
    out_v,
    weights,
    k_v,
    v_v,
    vt_v,
    nodes,
    left,
    total,
    lift,
    landed,
    tok_ref,
    tab_ref,
    table_pad,
    load_sem,
    small_sem,
    out_sem,
    send_sem,
    recv_sem,
):
    head_count, block_count, level_count, table_count, shards, device_bits = sizes
    block_bits = BLOCK.bit_length() - 1
    local_bits = block_count.bit_length() - 1
    padded = round_up(level_count, 8)
    me = lax.axis_index("ctx")

    def load(array_id, head_id):
        source = (k_hbm, v_hbm, q_hbm)[array_id]
        target = (k_v, v_v, q_v)[array_id]
        column = pl.multiple_of(head_id * WIDTH, WIDTH)
        return pltpu.make_async_copy(
            source.at[:, pl.ds(column, WIDTH)], target.at[head_id], load_sem.at[array_id, head_id]
        )

    tokens_in = pltpu.make_async_copy(tok_hbm, tok_ref, small_sem.at[0])
    table_in = pltpu.make_async_copy(tab_hbm, tab_ref, small_sem.at[1])
    tokens_in.start()
    table_in.start()
    for head_id in range(head_count):
        load(0, head_id).start()
        load(1, head_id).start()
    for head_id in range(head_count):
        load(2, head_id).start()

    if shards > 1:
        barrier = pltpu.get_barrier_semaphore()

        @pl.when(me > 0)
        def _():
            pl.semaphore_signal(
                barrier, inc=1, device_id={"ctx": me - 1}, device_id_type=pl.DeviceIdType.MESH
            )

    level_row = lax.broadcasted_iota(jnp.int32, (padded, WIDTH), 0)
    scale = jnp.zeros((padded, WIDTH), jnp.float32)
    for level_id in range(level_count):
        scale = jnp.where(level_row == level_id, level_constant(level_id), scale)
    table_rows = []
    table_pad[...] = jnp.zeros_like(table_pad)
    tokens_in.wait()
    table_in.wait()
    for head_id in range(head_count):
        table_pad[0:level_count, 0:table_count] = tab_ref[:, head_id, :]
        table_rows.append(table_pad[...] * scale)
    table_all = jnp.concatenate(table_rows, axis=0)
    high = table_all.astype(jnp.bfloat16)
    rest = table_all - high.astype(jnp.float32)
    middle = rest.astype(jnp.bfloat16)
    low = (rest - middle.astype(jnp.float32)).astype(jnp.bfloat16)
    split = jnp.concatenate([high, middle, low], axis=0)
    rows = head_count * padded

    def weigh(block, carry):
        tokens = jnp.concatenate(
            [tok_ref[pl.ds(2 * block, 1), :], tok_ref[pl.ds(2 * block + 1, 1), :]], axis=1
        )
        picks = lax.broadcasted_iota(jnp.int32, (WIDTH, BLOCK), 0) == tokens
        one_hot = jnp.where(picks, 1.0, 0.0).astype(jnp.bfloat16)
        parts = jnp.dot(split, one_hot, preferred_element_type=jnp.float32)
        weights[block] = parts[0:rows] + parts[rows : 2 * rows] + parts[2 * rows :]
        return carry

    lax.fori_loop(0, block_count, weigh, 0)

    def remote_copy(source, bit, head_id):
        return pltpu.make_async_remote_copy(
            src_ref=source,
            dst_ref=landed.at[bit, head_id],
            send_sem=send_sem.at[bit, head_id],
            recv_sem=recv_sem.at[bit, head_id],
            device_id={"ctx": me + 1},
            device_id_type=pl.DeviceIdType.MESH,
        )

    def has_bit(bit):
        return lax.rem(lax.div(me, 2**bit), 2) == 1

    def ends_span(bit):
        return lax.rem(me, 2**bit) == 2**bit - 1

    def is_source(bit):
        return jnp.logical_and(ends_span(bit), jnp.logical_not(has_bit(bit)))

    def is_relay(bit):
        return jnp.logical_and(has_bit(bit), jnp.logical_not(ends_span(bit)))

    if shards > 1:

        @pl.when(me < shards - 1)
        def _():
            pl.semaphore_wait(barrier, 1)

    def states(head_id, carry):
        load(0, head_id).wait()
        load(1, head_id).wait()

        def turn(block):
            span = pl.ds(block * BLOCK, BLOCK)
            value_t = jnp.transpose(v_v[head_id, span, :])
            vt_v[head_id, :, span] = value_t
            return value_t

        value_next = turn(0)
        for block in range(block_count):
            span = pl.ds(block * BLOCK, BLOCK)
            value_t = value_next
            if block + 1 < block_count:
                value_next = turn(block + 1)
            state = jnp.dot(value_t, k_v[head_id, span, :], preferred_element_type=jnp.float32)
            bit = 0
            while block >> bit & 1:
                state = left[bit] + state
                bit += 1
            if bit < local_bits:
                left[bit] = state
                nodes[head_id, node_index(block_count, bit, block >> (bit + 1))] = state.astype(
                    jnp.bfloat16
                )
            else:
                total[head_id] = state
        for bit in range(device_bits):

            @pl.when(jnp.logical_not(has_bit(bit)))
            def _(bit=bit):
                landed[bit, head_id] = jnp.zeros((WIDTH, WIDTH), jnp.float32)

        if shards > 1:

            @pl.when(is_source(0))
            def _():
                remote_copy(total.at[head_id], 0, head_id).start()

        return carry

    lax.fori_loop(0, head_count, states, 0)

    def service(bit, head_id):
        @pl.when(jnp.logical_and(has_bit(bit), me < shards - 1))
        def _():
            remote_copy(total.at[head_id], bit, head_id).wait_recv()

        @pl.when(is_relay(bit))
        def _():
            remote_copy(landed.at[bit, head_id], bit, head_id).start()

        if bit + 1 < device_bits:

            @pl.when(jnp.logical_and(ends_span(bit + 1), me < shards - 1))
            def _():
                base = total[head_id] if bit == 0 else lift[bit - 1, head_id]
                lift[bit, head_id] = base + landed[bit, head_id]

            @pl.when(is_source(bit + 1))
            def _():
                remote_copy(lift.at[bit, head_id], bit + 1, head_id).start()

    segment = block_count // head_count if block_count % head_count == 0 else 0

    def weight_row(block, head_id, level_id):
        return weights[block, pl.ds(head_id * padded + level_id, 1), :]

    def inside(head_id, carry):
        load(2, head_id).wait()

        def levels_of(block):
            return [bit for bit in range(local_bits) if block >> bit & 1]

        def multiply(block):
            span = pl.ds(block * BLOCK, BLOCK)
            stack = [k_v[head_id, span, :]] + [
                nodes[head_id, node_index(block_count, bit, block >> (bit + 1))]
                for bit in levels_of(block)
            ]
            return lax.dot_general(
                jnp.concatenate(stack, axis=0),
                q_v[head_id, span, :],
                NT,
                preferred_element_type=jnp.float32,
            )

        product_next = multiply(0)
        for block in range(block_count):
            if segment and block % segment == 0:
                for bit in range(min(device_bits, head_count)):

                    @pl.when(head_id == bit)
                    def _(bit=bit, block=block):
                        service(bit, block // segment)

            span = pl.ds(block * BLOCK, BLOCK)
            bits = levels_of(block)
            product = product_next
            if block + 1 < block_count:
                product_next = multiply(block + 1)
            level_rows = [
                weight_row(block, head_id, level_id) for level_id in range(block_bits + 1)
            ]
            first = pair_tile([row[:, :HALF] for row in level_rows])
            second = pair_tile([row[:, HALF:] for row in level_rows])
            top = jnp.concatenate(
                [
                    (product[:HALF, :HALF] * first).astype(jnp.bfloat16),
                    (product[:HALF, HALF:] * level_rows[block_bits][:, HALF:]).astype(jnp.bfloat16),
                ],
                axis=1,
            )
            bottom = jnp.concatenate(
                [
                    jnp.zeros((HALF, HALF), jnp.bfloat16),
                    (product[HALF:BLOCK, HALF:] * second).astype(jnp.bfloat16),
                ],
                axis=1,
            )
            weighted = jnp.concatenate([top, bottom], axis=0)
            result = jnp.dot(vt_v[head_id, :, span], weighted, preferred_element_type=jnp.float32)
            for place, bit in enumerate(bits):
                begin = BLOCK + place * WIDTH
                result = result + product[begin : begin + WIDTH] * weight_row(
                    block, head_id, block_bits + 1 + bit
                )
            acc[head_id, block] = result
        return carry

    lax.fori_loop(0, head_count, inside, 0)
    for bit in range(head_count if segment else 0, device_bits):
        for head_id in range(head_count):
            service(bit, head_id)

    first_level = BLOCK.bit_length() + block_count.bit_length() - 1
    chunk = max(1, block_count // 4)

    def write(head_id, part):
        column = pl.multiple_of(head_id * WIDTH, WIDTH)
        lines = pl.ds(part * chunk * BLOCK, chunk * BLOCK)
        return pltpu.make_async_copy(
            out_v.at[head_id, lines, :],
            out_hbm.at[lines, pl.ds(column, WIDTH)],
            out_sem.at[head_id, part],
        )

    def finish(head_id, carry):
        if device_bits:

            @pl.when(me == shards - 1)
            def _():
                for bit in range(device_bits):
                    remote_copy(total.at[head_id], bit, head_id).wait_recv()

            lines = jnp.concatenate(
                [landed[bit, head_id].astype(jnp.bfloat16) for bit in range(device_bits)], axis=0
            )

        def multiply(block):
            if not device_bits:
                return None
            return lax.dot_general(
                lines,
                q_v[head_id, pl.ds(block * BLOCK, BLOCK), :],
                NT,
                preferred_element_type=jnp.float32,
            )

        product_next = multiply(0)
        for block in range(block_count):
            product = product_next
            if block + 1 < block_count:
                product_next = multiply(block + 1)
            result = acc[head_id, block]
            for bit in range(device_bits):
                row = weights[block, pl.ds(head_id * padded + first_level + bit, 1), :]
                result = result + product[bit * WIDTH : (bit + 1) * WIDTH] * row
            out_v[head_id, pl.ds(block * BLOCK, BLOCK), :] = jnp.transpose(
                result.astype(jnp.bfloat16)
            )
            if block % chunk == chunk - 1:
                write(head_id, block // chunk).start()
        return carry

    lax.fori_loop(0, head_count, finish, 0)
    for head_id in range(head_count):
        for part in range(block_count // chunk):
            write(head_id, part).wait()
    for bit in range(device_bits):

        @pl.when(jnp.logical_or(is_source(bit), is_relay(bit)))
        def _(bit=bit):
            for head_id in range(head_count):
                remote_copy(total.at[head_id], bit, head_id).wait_send()


def body(queries, key_vectors, value_vectors, token_rows, weight_table):
    table_count, head_count, level_count = weight_table.shape
    token_count = queries.shape[0]
    block_count = token_count // BLOCK
    shards = lax.axis_size("ctx")
    device_bits = shards.bit_length() - 1
    padded = round_up(level_count, 8)
    slots = max(1, device_bits)
    sizes = (head_count, block_count, level_count, table_count, shards, device_bits)
    hbm = pl.BlockSpec(memory_space=pl.ANY)
    wide = (head_count, token_count, WIDTH)
    state = (WIDTH, WIDTH)
    return pl.pallas_call(
        functools.partial(kernel, sizes),
        out_shape=jax.ShapeDtypeStruct(queries.shape, jnp.bfloat16),
        in_specs=[hbm] * 5,
        out_specs=hbm,
        scratch_shapes=[
            pltpu.VMEM((head_count, block_count, WIDTH, BLOCK), jnp.float32),
            pltpu.VMEM(wide, jnp.bfloat16),
            pltpu.VMEM(wide, jnp.bfloat16),
            pltpu.VMEM((block_count, head_count * padded, BLOCK), jnp.float32),
            pltpu.VMEM(wide, jnp.bfloat16),
            pltpu.VMEM(wide, jnp.bfloat16),
            pltpu.VMEM((head_count, WIDTH, token_count), jnp.bfloat16),
            pltpu.VMEM((head_count, max(1, block_count - 1)) + state, jnp.bfloat16),
            pltpu.VMEM((max(1, block_count.bit_length() - 1),) + state, jnp.float32),
            pltpu.VMEM((head_count,) + state, jnp.float32),
            pltpu.VMEM((slots, head_count) + state, jnp.float32),
            pltpu.VMEM((slots, head_count) + state, jnp.float32),
            pltpu.VMEM((token_count // WIDTH, WIDTH), jnp.int32),
            pltpu.VMEM((level_count, head_count, table_count), jnp.float32),
            pltpu.VMEM((padded, WIDTH), jnp.float32),
            pltpu.SemaphoreType.DMA((3, head_count)),
            pltpu.SemaphoreType.DMA((2,)),
            pltpu.SemaphoreType.DMA((head_count, 4)),
            pltpu.SemaphoreType.DMA((slots, head_count)),
            pltpu.SemaphoreType.DMA((slots, head_count)),
        ],
        compiler_params=pltpu.CompilerParams(
            collective_id=0, has_side_effects=True, vmem_limit_bytes=46 * 1024 * 1024
        ),
        cost_estimate=pl.CostEstimate(
            flops=10 * token_count * head_count * WIDTH * BLOCK,
            bytes_accessed=6 * token_count * head_count * WIDTH,
            transcendentals=0,
        ),
    )(
        *[
            pltpu.with_memory_space_constraint(operand, pltpu.HBM)
            for operand in (
                queries,
                key_vectors,
                value_vectors,
                token_rows.reshape(token_count // WIDTH, WIDTH),
                weight_table.transpose(2, 1, 0),
            )
        ]
    )


def solution(mesh):
    placed = (
        P(("groups", "ctx"), "head"),
        P(("groups", "ctx"), "head"),
        P(("groups", "ctx"), "head"),
        P(("groups", "ctx")),
        P(None, "head", None),
    )
    return jax.shard_map(
        body, mesh=mesh, in_specs=placed, out_specs=P(("groups", "ctx"), "head"), check_vma=False
    )
```

```python
import functools

import jax
import jax.numpy as jnp
from jax import lax
from jax.experimental import pallas as pl
from jax.experimental.pallas import tpu as pltpu
from jax.sharding import PartitionSpec as P

BLOCK = 256
HALF = 128
WIDTH = 128
NT = (((1,), (1,)), ((), ()))


def level_constant(level_id):
    return 1.0 if level_id == 0 else 2.0 ** (-(level_id - 1) / 2.0)


def round_up(size, unit):
    return (size + unit - 1) // unit * unit


def node_index(block_count, bit, group):
    start = sum(block_count >> (low + 1) for low in range(bit))
    return start + group


def pair_tile(weight_rows):
    near_row = lax.broadcasted_iota(jnp.int32, (8, HALF), 0)
    near_lane = lax.broadcasted_iota(jnp.int32, (8, HALF), 1)
    near_target = near_lane & 7
    near_xor = near_row ^ near_target
    near = jnp.where(near_xor >= 1, weight_rows[1], weight_rows[0])
    near = jnp.where(near_xor >= 2, weight_rows[2], near)
    near = jnp.where(near_xor >= 4, weight_rows[3], near)
    near = jnp.where(near_row <= near_target, near, 0.0)
    far_row = lax.broadcasted_iota(jnp.int32, (16, HALF), 0)
    far_target = lax.broadcasted_iota(jnp.int32, (16, HALF), 1) >> 3
    far_xor = far_row ^ far_target
    far = jnp.where(far_xor >= 2, weight_rows[5], weight_rows[4])
    far = jnp.where(far_xor >= 4, weight_rows[6], far)
    far = jnp.where(far_xor >= 8, weight_rows[7], far)
    far = jnp.where(far_row <= far_target, far, 0.0)
    lane_group = near_lane >> 3
    return jnp.concatenate(
        [jnp.where(lane_group == row, near, far[row : row + 1]) for row in range(16)], axis=0
    )


def kernel(
    sizes,
    q_hbm,
    k_hbm,
    v_hbm,
    tok_hbm,
    tab_hbm,
    acc,
    q_v,
    remote,
    weights,
    k_v,
    v_v,
    vt_v,
    nodes,
    left,
    total,
    lift,
    landed,
    tok_ref,
    tab_ref,
    table_pad,
    load_sem,
    small_sem,
    send_sem,
    recv_sem,
):
    head_count, block_count, level_count, table_count, shards, device_bits = sizes
    block_bits = BLOCK.bit_length() - 1
    local_bits = block_count.bit_length() - 1
    padded = round_up(level_count, 8)
    me = lax.axis_index("ctx")

    def load(array_id, head_id):
        source = (k_hbm, v_hbm, q_hbm)[array_id]
        target = (k_v, v_v, q_v)[array_id]
        column = pl.multiple_of(head_id * WIDTH, WIDTH)
        return pltpu.make_async_copy(
            source.at[:, pl.ds(column, WIDTH)], target.at[head_id], load_sem.at[array_id, head_id]
        )

    tokens_in = pltpu.make_async_copy(tok_hbm, tok_ref, small_sem.at[0])
    table_in = pltpu.make_async_copy(tab_hbm, tab_ref, small_sem.at[1])
    tokens_in.start()
    table_in.start()
    for head_id in range(head_count):
        load(0, head_id).start()
        load(1, head_id).start()
    for head_id in range(head_count):
        load(2, head_id).start()

    if shards > 1:
        barrier = pltpu.get_barrier_semaphore()

        @pl.when(me > 0)
        def _():
            pl.semaphore_signal(
                barrier, inc=1, device_id={"ctx": me - 1}, device_id_type=pl.DeviceIdType.MESH
            )

    level_row = lax.broadcasted_iota(jnp.int32, (padded, WIDTH), 0)
    scale = jnp.zeros((padded, WIDTH), jnp.float32)
    for level_id in range(level_count):
        scale = jnp.where(level_row == level_id, level_constant(level_id), scale)
    table_rows = []
    table_pad[...] = jnp.zeros_like(table_pad)
    tokens_in.wait()
    table_in.wait()
    for head_id in range(head_count):
        table_pad[0:level_count, 0:table_count] = tab_ref[:, head_id, :]
        table_rows.append(table_pad[...] * scale)
    table_all = jnp.concatenate(table_rows, axis=0)
    high = table_all.astype(jnp.bfloat16)
    rest = table_all - high.astype(jnp.float32)
    middle = rest.astype(jnp.bfloat16)
    low = (rest - middle.astype(jnp.float32)).astype(jnp.bfloat16)
    split = jnp.concatenate([high, middle, low], axis=0)
    rows = head_count * padded

    def weigh(block, carry):
        tokens = jnp.concatenate(
            [tok_ref[pl.ds(2 * block, 1), :], tok_ref[pl.ds(2 * block + 1, 1), :]], axis=1
        )
        picks = lax.broadcasted_iota(jnp.int32, (WIDTH, BLOCK), 0) == tokens
        one_hot = jnp.where(picks, 1.0, 0.0).astype(jnp.bfloat16)
        parts = jnp.dot(split, one_hot, preferred_element_type=jnp.float32)
        weights[block] = parts[0:rows] + parts[rows : 2 * rows] + parts[2 * rows :]
        return carry

    lax.fori_loop(0, block_count, weigh, 0)

    def remote_copy(source, bit, head_id):
        return pltpu.make_async_remote_copy(
            src_ref=source,
            dst_ref=landed.at[bit, head_id],
            send_sem=send_sem.at[bit, head_id],
            recv_sem=recv_sem.at[bit, head_id],
            device_id={"ctx": me + 1},
            device_id_type=pl.DeviceIdType.MESH,
        )

    def has_bit(bit):
        return lax.rem(lax.div(me, 2**bit), 2) == 1

    def ends_span(bit):
        return lax.rem(me, 2**bit) == 2**bit - 1

    def is_source(bit):
        return jnp.logical_and(ends_span(bit), jnp.logical_not(has_bit(bit)))

    def is_relay(bit):
        return jnp.logical_and(has_bit(bit), jnp.logical_not(ends_span(bit)))

    if shards > 1:

        @pl.when(me < shards - 1)
        def _():
            pl.semaphore_wait(barrier, 1)

    def states(head_id, carry):
        load(0, head_id).wait()
        load(1, head_id).wait()

        def turn(block):
            span = pl.ds(block * BLOCK, BLOCK)
            value_t = jnp.transpose(v_v[head_id, span, :])
            vt_v[head_id, :, span] = value_t
            return value_t

        value_next = turn(0)
        for block in range(block_count):
            span = pl.ds(block * BLOCK, BLOCK)
            value_t = value_next
            if block + 1 < block_count:
                value_next = turn(block + 1)
            state = jnp.dot(value_t, k_v[head_id, span, :], preferred_element_type=jnp.float32)
            bit = 0
            while block >> bit & 1:
                state = left[bit] + state
                bit += 1
            if bit < local_bits:
                left[bit] = state
                nodes[head_id, node_index(block_count, bit, block >> (bit + 1))] = state.astype(
                    jnp.bfloat16
                )
            else:
                total[head_id] = state
        for bit in range(device_bits):

            @pl.when(jnp.logical_not(has_bit(bit)))
            def _(bit=bit):
                landed[bit, head_id] = jnp.zeros((WIDTH, WIDTH), jnp.float32)

        if shards > 1:

            @pl.when(is_source(0))
            def _():
                remote_copy(total.at[head_id], 0, head_id).start()

        return carry

    lax.fori_loop(0, head_count, states, 0)

    def service(bit, head_id):
        @pl.when(jnp.logical_and(has_bit(bit), me < shards - 1))
        def _():
            remote_copy(total.at[head_id], bit, head_id).wait_recv()

        @pl.when(is_relay(bit))
        def _():
            remote_copy(landed.at[bit, head_id], bit, head_id).start()

        if bit + 1 < device_bits:

            @pl.when(jnp.logical_and(ends_span(bit + 1), me < shards - 1))
            def _():
                base = total[head_id] if bit == 0 else lift[bit - 1, head_id]
                lift[bit, head_id] = base + landed[bit, head_id]

            @pl.when(is_source(bit + 1))
            def _():
                remote_copy(lift.at[bit, head_id], bit + 1, head_id).start()

    segment = block_count // head_count if block_count % head_count == 0 else 0

    def weight_row(block, head_id, level_id):
        return weights[block, pl.ds(head_id * padded + level_id, 1), :]

    def inside(head_id, carry):
        load(2, head_id).wait()

        def levels_of(block):
            return [bit for bit in range(local_bits) if block >> bit & 1]

        def multiply(block):
            span = pl.ds(block * BLOCK, BLOCK)
            stack = [k_v[head_id, span, :]] + [
                nodes[head_id, node_index(block_count, bit, block >> (bit + 1))]
                for bit in levels_of(block)
            ]
            return lax.dot_general(
                jnp.concatenate(stack, axis=0),
                q_v[head_id, span, :],
                NT,
                preferred_element_type=jnp.float32,
            )

        product_next = multiply(0)
        for block in range(block_count):
            if segment and block % segment == 0:
                for bit in range(min(device_bits, head_count - 1)):

                    @pl.when(head_id == bit + 1)
                    def _(bit=bit, block=block):
                        service(bit, block // segment)

            span = pl.ds(block * BLOCK, BLOCK)
            bits = levels_of(block)
            product = product_next
            if block + 1 < block_count:
                product_next = multiply(block + 1)
            level_rows = [
                weight_row(block, head_id, level_id) for level_id in range(block_bits + 1)
            ]
            first = pair_tile([row[:, :HALF] for row in level_rows])
            second = pair_tile([row[:, HALF:] for row in level_rows])
            top = jnp.concatenate(
                [
                    (product[:HALF, :HALF] * first).astype(jnp.bfloat16),
                    (product[:HALF, HALF:] * level_rows[block_bits][:, HALF:]).astype(jnp.bfloat16),
                ],
                axis=1,
            )
            bottom = jnp.concatenate(
                [
                    jnp.zeros((HALF, HALF), jnp.bfloat16),
                    (product[HALF:BLOCK, HALF:] * second).astype(jnp.bfloat16),
                ],
                axis=1,
            )
            weighted = jnp.concatenate([top, bottom], axis=0)
            result = jnp.dot(vt_v[head_id, :, span], weighted, preferred_element_type=jnp.float32)
            for place, bit in enumerate(bits):
                begin = BLOCK + place * WIDTH
                result = result + product[begin : begin + WIDTH] * weight_row(
                    block, head_id, block_bits + 1 + bit
                )
            acc[head_id, block] = result
        return carry

    lax.fori_loop(0, head_count, inside, 0)
    for bit in range(min(device_bits, head_count - 1) if segment else 0, device_bits):
        for head_id in range(head_count):
            service(bit, head_id)

    if shards > 1:

        @pl.when(me == shards - 1)
        def _():
            for bit in range(device_bits):
                for head_id in range(head_count):
                    remote_copy(total.at[head_id], bit, head_id).wait_recv()

    for bit in range(device_bits):
        for head_id in range(head_count):
            remote[head_id, bit * WIDTH : (bit + 1) * WIDTH, :] = landed[bit, head_id].astype(
                jnp.bfloat16
            )
    for bit in range(device_bits):

        @pl.when(jnp.logical_or(is_source(bit), is_relay(bit)))
        def _(bit=bit):
            for head_id in range(head_count):
                remote_copy(total.at[head_id], bit, head_id).wait_send()


def finish_kernel(sizes, acc, q_v, remote, weights, out_hbm, out_v, out_sem):
    head_count, block_count, level_count, table_count, shards, device_bits = sizes
    first_level = BLOCK.bit_length() + block_count.bit_length() - 1
    padded = round_up(level_count, 8)
    chunk = max(1, block_count // 4)

    def write(head_id, part):
        column = pl.multiple_of(head_id * WIDTH, WIDTH)
        lines = pl.ds(part * chunk * BLOCK, chunk * BLOCK)
        return pltpu.make_async_copy(
            out_v.at[head_id, lines, :],
            out_hbm.at[lines, pl.ds(column, WIDTH)],
            out_sem.at[head_id, part],
        )

    def finish(head_id, carry):
        def multiply(block):
            if not device_bits:
                return None
            return lax.dot_general(
                remote[head_id],
                q_v[head_id, pl.ds(block * BLOCK, BLOCK), :],
                NT,
                preferred_element_type=jnp.float32,
            )

        product_next = multiply(0)
        for block in range(block_count):
            product = product_next
            if block + 1 < block_count:
                product_next = multiply(block + 1)
            result = acc[head_id, block]
            for bit in range(device_bits):
                row = weights[block, pl.ds(head_id * padded + first_level + bit, 1), :]
                result = result + product[bit * WIDTH : (bit + 1) * WIDTH] * row
            out_v[head_id, pl.ds(block * BLOCK, BLOCK), :] = jnp.transpose(
                result.astype(jnp.bfloat16)
            )
            if block % chunk == chunk - 1:
                write(head_id, block // chunk).start()
        return carry

    lax.fori_loop(0, head_count, finish, 0)
    for head_id in range(head_count):
        for part in range(block_count // chunk):
            write(head_id, part).wait()


def body(queries, key_vectors, value_vectors, token_rows, weight_table):
    table_count, head_count, level_count = weight_table.shape
    token_count = queries.shape[0]
    block_count = token_count // BLOCK
    shards = lax.axis_size("ctx")
    device_bits = shards.bit_length() - 1
    padded = round_up(level_count, 8)
    slots = max(1, device_bits)
    sizes = (head_count, block_count, level_count, table_count, shards, device_bits)
    hbm = pl.BlockSpec(memory_space=pltpu.HBM)
    vmem = pl.BlockSpec(memory_space=pltpu.VMEM)
    wide = (head_count, token_count, WIDTH)
    state = (WIDTH, WIDTH)
    acc, q_v, remote, weights = pl.pallas_call(
        functools.partial(kernel, sizes),
        out_shape=[
            jax.ShapeDtypeStruct((head_count, block_count, WIDTH, BLOCK), jnp.float32),
            jax.ShapeDtypeStruct(wide, jnp.bfloat16),
            jax.ShapeDtypeStruct((head_count, slots * WIDTH, WIDTH), jnp.bfloat16),
            jax.ShapeDtypeStruct((block_count, head_count * padded, BLOCK), jnp.float32),
        ],
        in_specs=[hbm] * 5,
        out_specs=[vmem] * 4,
        scratch_shapes=[
            pltpu.VMEM(wide, jnp.bfloat16),
            pltpu.VMEM(wide, jnp.bfloat16),
            pltpu.VMEM((head_count, WIDTH, token_count), jnp.bfloat16),
            pltpu.VMEM((head_count, max(1, block_count - 1)) + state, jnp.bfloat16),
            pltpu.VMEM((max(1, block_count.bit_length() - 1),) + state, jnp.float32),
            pltpu.VMEM((head_count,) + state, jnp.float32),
            pltpu.VMEM((slots, head_count) + state, jnp.float32),
            pltpu.VMEM((slots, head_count) + state, jnp.float32),
            pltpu.VMEM((token_count // WIDTH, WIDTH), jnp.int32),
            pltpu.VMEM((level_count, head_count, table_count), jnp.float32),
            pltpu.VMEM((padded, WIDTH), jnp.float32),
            pltpu.SemaphoreType.DMA((3, head_count)),
            pltpu.SemaphoreType.DMA((2,)),
            pltpu.SemaphoreType.DMA((slots, head_count)),
            pltpu.SemaphoreType.DMA((slots, head_count)),
        ],
        compiler_params=pltpu.CompilerParams(
            collective_id=0, has_side_effects=True, vmem_limit_bytes=32 * 1024 * 1024
        ),
        cost_estimate=pl.CostEstimate(
            flops=10 * token_count * head_count * WIDTH * BLOCK,
            bytes_accessed=6 * token_count * head_count * WIDTH,
            transcendentals=0,
        ),
    )(
        *[
            pltpu.with_memory_space_constraint(operand, pltpu.HBM)
            for operand in (
                queries,
                key_vectors,
                value_vectors,
                token_rows.reshape(token_count // WIDTH, WIDTH),
                weight_table.transpose(2, 1, 0),
            )
        ]
    )
    return pl.pallas_call(
        functools.partial(finish_kernel, sizes),
        out_shape=jax.ShapeDtypeStruct(queries.shape, jnp.bfloat16),
        in_specs=[vmem] * 4,
        out_specs=hbm,
        scratch_shapes=[
            pltpu.VMEM(wide, jnp.bfloat16),
            pltpu.SemaphoreType.DMA((head_count, 4)),
        ],
        compiler_params=pltpu.CompilerParams(vmem_limit_bytes=32 * 1024 * 1024),
        cost_estimate=pl.CostEstimate(
            flops=4 * token_count * head_count * WIDTH * WIDTH,
            bytes_accessed=2 * token_count * head_count * WIDTH,
            transcendentals=0,
        ),
    )(acc, q_v, remote, weights)


def solution(mesh):
    placed = (
        P(("groups", "ctx"), "head"),
        P(("groups", "ctx"), "head"),
        P(("groups", "ctx"), "head"),
        P(("groups", "ctx")),
        P(None, "head", None),
    )
    return jax.shard_map(
        body, mesh=mesh, in_specs=placed, out_specs=P(("groups", "ctx"), "head"), check_vma=False
    )
```

```python
import functools

import jax
import jax.numpy as jnp
from jax import lax
from jax.experimental import pallas as pl
from jax.experimental.pallas import tpu as pltpu
from jax.sharding import PartitionSpec as P

BLOCK = 256
HALF = 128
WIDTH = 128
NT = (((1,), (1,)), ((), ()))


def level_constant(level_id):
    return 1.0 if level_id == 0 else 2.0 ** (-(level_id - 1) / 2.0)


def round_up(size, unit):
    return (size + unit - 1) // unit * unit


def node_index(block_count, bit, group):
    start = sum(block_count >> (low + 1) for low in range(bit))
    return start + group


def pair_tile(weight_rows):
    source = lax.broadcasted_iota(jnp.int32, (8, HALF), 0)
    target = lax.broadcasted_iota(jnp.int32, (8, HALF), 1)
    near_target = target & 7
    near_xor = source ^ near_target
    near = jnp.where(near_xor >= 1, weight_rows[1], weight_rows[0])
    near = jnp.where(near_xor >= 2, weight_rows[2], near)
    near = jnp.where(near_xor >= 4, weight_rows[3], near)
    near = jnp.where(source <= near_target, near, 0.0)
    spans = [jnp.zeros((8, HALF), jnp.float32)]
    for level_id in (7, 6, 5, 4):
        wider = []
        for index, span in enumerate(spans):
            right = target >> (level_id - 1) == 2 * index + 1
            wider += [jnp.where(right, weight_rows[level_id], span), span]
        spans = wider
    return jnp.concatenate(
        [jnp.where(target >> 3 == row, near, span) for row, span in enumerate(spans)], axis=0
    )


def kernel(
    sizes,
    q_hbm,
    k_hbm,
    v_hbm,
    tok_hbm,
    tab_hbm,
    acc,
    q_v,
    remote,
    weights,
    k_v,
    v_v,
    vt_v,
    nodes,
    left,
    total,
    lift,
    landed,
    tok_ref,
    tab_ref,
    table_pad,
    load_sem,
    small_sem,
    send_sem,
    recv_sem,
):
    head_count, block_count, level_count, table_count, shards, device_bits = sizes
    block_bits = BLOCK.bit_length() - 1
    local_bits = block_count.bit_length() - 1
    padded = round_up(level_count, 8)
    me = lax.axis_index("ctx")

    def load(array_id, head_id):
        source = (k_hbm, v_hbm, q_hbm)[array_id]
        target = (k_v, v_v, q_v)[array_id]
        column = pl.multiple_of(head_id * WIDTH, WIDTH)
        return pltpu.make_async_copy(
            source.at[:, pl.ds(column, WIDTH)], target.at[head_id], load_sem.at[array_id, head_id]
        )

    tokens_in = pltpu.make_async_copy(tok_hbm, tok_ref, small_sem.at[0])
    table_in = pltpu.make_async_copy(tab_hbm, tab_ref, small_sem.at[1])
    tokens_in.start()
    table_in.start()
    for head_id in range(min(2, head_count)):
        load(0, head_id).start()
        load(1, head_id).start()

    if shards > 1:
        barrier = pltpu.get_barrier_semaphore()

        @pl.when(me > 0)
        def _():
            pl.semaphore_signal(
                barrier, inc=1, device_id={"ctx": me - 1}, device_id_type=pl.DeviceIdType.MESH
            )

    level_row = lax.broadcasted_iota(jnp.int32, (padded, WIDTH), 0)
    scale = jnp.zeros((padded, WIDTH), jnp.float32)
    for level_id in range(level_count):
        scale = jnp.where(level_row == level_id, level_constant(level_id), scale)
    table_rows = []
    table_pad[...] = jnp.zeros_like(table_pad)
    tokens_in.wait()
    table_in.wait()
    for head_id in range(head_count):
        table_pad[0:level_count, 0:table_count] = tab_ref[:, head_id, :]
        table_rows.append(table_pad[...] * scale)
    table_all = jnp.concatenate(table_rows, axis=0)
    high = table_all.astype(jnp.bfloat16)
    rest = table_all - high.astype(jnp.float32)
    middle = rest.astype(jnp.bfloat16)
    low = (rest - middle.astype(jnp.float32)).astype(jnp.bfloat16)
    split = jnp.concatenate([high, middle, low], axis=0)
    rows = head_count * padded

    def weigh(block):
        tokens = jnp.concatenate(
            [tok_ref[pl.ds(2 * block, 1), :], tok_ref[pl.ds(2 * block + 1, 1), :]], axis=1
        )
        picks = lax.broadcasted_iota(jnp.int32, (WIDTH, BLOCK), 0) == tokens
        one_hot = jnp.where(picks, 1.0, 0.0).astype(jnp.bfloat16)
        parts = jnp.dot(split, one_hot, preferred_element_type=jnp.float32)
        whole = parts[0:rows] + parts[rows : 2 * rows] + parts[2 * rows :]
        for head_id in range(head_count):
            weights[block, head_id] = whole[head_id * padded : (head_id + 1) * padded]

    def remote_copy(source, bit, head_id):
        return pltpu.make_async_remote_copy(
            src_ref=source,
            dst_ref=landed.at[bit, head_id],
            send_sem=send_sem.at[bit, head_id],
            recv_sem=recv_sem.at[bit, head_id],
            device_id={"ctx": me + 1},
            device_id_type=pl.DeviceIdType.MESH,
        )

    def has_bit(bit):
        return lax.rem(lax.div(me, 2**bit), 2) == 1

    def ends_span(bit):
        return lax.rem(me, 2**bit) == 2**bit - 1

    def is_source(bit):
        return jnp.logical_and(ends_span(bit), jnp.logical_not(has_bit(bit)))

    def is_relay(bit):
        return jnp.logical_and(has_bit(bit), jnp.logical_not(ends_span(bit)))

    if shards > 1:

        @pl.when(me < shards - 1)
        def _():
            pl.semaphore_wait(barrier, 1)

    def states(head_id, carry):
        load(0, head_id).wait()
        load(1, head_id).wait()

        @pl.when(head_id + 2 < head_count)
        def _():
            load(0, head_id + 2).start()
            load(1, head_id + 2).start()

        load(2, head_id).start()

        def turn(block):
            span = pl.ds(block * BLOCK, BLOCK)
            value_t = jnp.transpose(v_v[head_id, span, :])
            vt_v[head_id, :, span] = value_t
            return value_t

        value_next = turn(0)
        for block in range(block_count):
            span = pl.ds(block * BLOCK, BLOCK)
            value_t = value_next
            if block + 1 < block_count:
                value_next = turn(block + 1)
            if block % head_count == head_count - 1:
                weigh(head_id * (block_count // head_count) + block // head_count)
            state = jnp.dot(value_t, k_v[head_id, span, :], preferred_element_type=jnp.float32)
            bit = 0
            while block >> bit & 1:
                state = left[bit] + state
                bit += 1
            if bit < local_bits:
                left[bit] = state
                nodes[head_id, node_index(block_count, bit, block >> (bit + 1))] = state.astype(
                    jnp.bfloat16
                )
            else:
                total[head_id] = state
        for bit in range(device_bits):

            @pl.when(jnp.logical_not(has_bit(bit)))
            def _(bit=bit):
                landed[bit, head_id] = jnp.zeros((WIDTH, WIDTH), jnp.float32)

        if shards > 1:

            @pl.when(is_source(0))
            def _():
                remote_copy(total.at[head_id], 0, head_id).start()

        return carry

    lax.fori_loop(0, head_count, states, 0)

    def service(bit, head_id):
        @pl.when(jnp.logical_and(has_bit(bit), me < shards - 1))
        def _():
            remote_copy(total.at[head_id], bit, head_id).wait_recv()

        @pl.when(is_relay(bit))
        def _():
            remote_copy(landed.at[bit, head_id], bit, head_id).start()

        if bit + 1 < device_bits:

            @pl.when(jnp.logical_and(ends_span(bit + 1), me < shards - 1))
            def _():
                base = total[head_id] if bit == 0 else lift[bit - 1, head_id]
                lift[bit, head_id] = base + landed[bit, head_id]

            @pl.when(is_source(bit + 1))
            def _():
                remote_copy(lift.at[bit, head_id], bit + 1, head_id).start()

    segment = block_count // 4
    due = sorted(
        (3 + 5 * bit + 2 * head_id, bit, head_id)
        for bit in range(device_bits)
        for head_id in range(head_count)
    )

    def weight_row(block, head_id, level_id):
        return weights[block, head_id, level_id : level_id + 1, :]

    def inside(head_id, carry):
        load(2, head_id).wait()

        def levels_of(block):
            return [bit for bit in range(local_bits) if block >> bit & 1]

        def multiply(block):
            span = pl.ds(block * BLOCK, BLOCK)
            stack = [k_v[head_id, span, :]] + [
                nodes[head_id, node_index(block_count, bit, block >> (bit + 1))]
                for bit in levels_of(block)
            ]
            return lax.dot_general(
                jnp.concatenate(stack, axis=0),
                q_v[head_id, span, :],
                NT,
                preferred_element_type=jnp.float32,
            )

        product_next = multiply(0)
        for block in range(block_count):
            if block % segment == 0:
                for point, bit, which in due:
                    if point % 4 == block // segment and point < 4 * head_count:

                        @pl.when(head_id == point // 4)
                        def _(bit=bit, which=which):
                            service(bit, which)

            span = pl.ds(block * BLOCK, BLOCK)
            bits = levels_of(block)
            product = product_next
            if block + 1 < block_count:
                product_next = multiply(block + 1)
            level_rows = [
                weight_row(block, head_id, level_id) for level_id in range(block_bits + 1)
            ]
            first = pair_tile([jnp.broadcast_to(row[:, :HALF], (8, HALF)) for row in level_rows])
            second = pair_tile([jnp.broadcast_to(row[:, HALF:], (8, HALF)) for row in level_rows])
            top = jnp.concatenate(
                [
                    (product[:HALF, :HALF] * first).astype(jnp.bfloat16),
                    (product[:HALF, HALF:] * level_rows[block_bits][:, HALF:]).astype(jnp.bfloat16),
                ],
                axis=1,
            )
            bottom = jnp.concatenate(
                [
                    jnp.zeros((HALF, HALF), jnp.bfloat16),
                    (product[HALF:BLOCK, HALF:] * second).astype(jnp.bfloat16),
                ],
                axis=1,
            )
            weighted = jnp.concatenate([top, bottom], axis=0)
            result = jnp.dot(vt_v[head_id, :, span], weighted, preferred_element_type=jnp.float32)
            for place, bit in enumerate(bits):
                begin = BLOCK + place * WIDTH
                result = result + product[begin : begin + WIDTH] * weight_row(
                    block, head_id, block_bits + 1 + bit
                )
            acc[head_id, block] = result
        return carry

    lax.fori_loop(0, head_count, inside, 0)
    for point, bit, head_id in due:
        if point >= 4 * head_count:
            service(bit, head_id)

    if shards > 1:

        @pl.when(me == shards - 1)
        def _():
            for bit in range(device_bits):
                for head_id in range(head_count):
                    remote_copy(total.at[head_id], bit, head_id).wait_recv()

    for bit in range(device_bits):
        for head_id in range(head_count):
            remote[head_id, bit * WIDTH : (bit + 1) * WIDTH, :] = landed[bit, head_id].astype(
                jnp.bfloat16
            )
    for bit in range(device_bits):

        @pl.when(jnp.logical_or(is_source(bit), is_relay(bit)))
        def _(bit=bit):
            for head_id in range(head_count):
                remote_copy(total.at[head_id], bit, head_id).wait_send()


def finish_kernel(sizes, acc, q_v, remote, weights, out_hbm, out_v, out_sem):
    head_count, block_count, level_count, table_count, shards, device_bits = sizes
    first_level = BLOCK.bit_length() + block_count.bit_length() - 1
    padded = round_up(level_count, 8)
    chunk = max(1, block_count // 4)

    def write(head_id, part):
        column = pl.multiple_of(head_id * WIDTH, WIDTH)
        lines = pl.ds(part * chunk * BLOCK, chunk * BLOCK)
        return pltpu.make_async_copy(
            out_v.at[head_id, lines, :],
            out_hbm.at[lines, pl.ds(column, WIDTH)],
            out_sem.at[head_id, part],
        )

    def finish(head_id, carry):
        def multiply(block):
            if not device_bits:
                return None
            return lax.dot_general(
                remote[head_id],
                q_v[head_id, pl.ds(block * BLOCK, BLOCK), :],
                NT,
                preferred_element_type=jnp.float32,
            )

        product_next = multiply(0)
        for block in range(block_count):
            product = product_next
            if block + 1 < block_count:
                product_next = multiply(block + 1)
            result = acc[head_id, block]
            for bit in range(device_bits):
                row = weights[block, head_id, first_level + bit : first_level + bit + 1, :]
                result = result + product[bit * WIDTH : (bit + 1) * WIDTH] * row
            out_v[head_id, pl.ds(block * BLOCK, BLOCK), :] = jnp.transpose(
                result.astype(jnp.bfloat16)
            )
            if block % chunk == chunk - 1:
                write(head_id, block // chunk).start()
        return carry

    lax.fori_loop(0, head_count, finish, 0)
    for head_id in range(head_count):
        for part in range(block_count // chunk):
            write(head_id, part).wait()


def body(queries, key_vectors, value_vectors, token_rows, weight_table):
    table_count, head_count, level_count = weight_table.shape
    token_count = queries.shape[0]
    block_count = token_count // BLOCK
    shards = lax.axis_size("ctx")
    device_bits = shards.bit_length() - 1
    padded = round_up(level_count, 8)
    slots = max(1, device_bits)
    sizes = (head_count, block_count, level_count, table_count, shards, device_bits)
    hbm = pl.BlockSpec(memory_space=pltpu.HBM)
    vmem = pl.BlockSpec(memory_space=pltpu.VMEM)
    wide = (head_count, token_count, WIDTH)
    state = (WIDTH, WIDTH)
    acc, q_v, remote, weights = pl.pallas_call(
        functools.partial(kernel, sizes),
        out_shape=[
            jax.ShapeDtypeStruct((head_count, block_count, WIDTH, BLOCK), jnp.float32),
            jax.ShapeDtypeStruct(wide, jnp.bfloat16),
            jax.ShapeDtypeStruct((head_count, slots * WIDTH, WIDTH), jnp.bfloat16),
            jax.ShapeDtypeStruct((block_count, head_count, padded, BLOCK), jnp.float32),
        ],
        in_specs=[hbm] * 5,
        out_specs=[vmem] * 4,
        scratch_shapes=[
            pltpu.VMEM(wide, jnp.bfloat16),
            pltpu.VMEM(wide, jnp.bfloat16),
            pltpu.VMEM((head_count, WIDTH, token_count), jnp.bfloat16),
            pltpu.VMEM((head_count, max(1, block_count - 1)) + state, jnp.bfloat16),
            pltpu.VMEM((max(1, block_count.bit_length() - 1),) + state, jnp.float32),
            pltpu.VMEM((head_count,) + state, jnp.float32),
            pltpu.VMEM((slots, head_count) + state, jnp.float32),
            pltpu.VMEM((slots, head_count) + state, jnp.float32),
            pltpu.VMEM((token_count // WIDTH, WIDTH), jnp.int32),
            pltpu.VMEM((level_count, head_count, table_count), jnp.float32),
            pltpu.VMEM((padded, WIDTH), jnp.float32),
            pltpu.SemaphoreType.DMA((3, head_count)),
            pltpu.SemaphoreType.DMA((2,)),
            pltpu.SemaphoreType.DMA((slots, head_count)),
            pltpu.SemaphoreType.DMA((slots, head_count)),
        ],
        compiler_params=pltpu.CompilerParams(
            collective_id=0, has_side_effects=True, vmem_limit_bytes=32 * 1024 * 1024
        ),
        cost_estimate=pl.CostEstimate(
            flops=10 * token_count * head_count * WIDTH * BLOCK,
            bytes_accessed=6 * token_count * head_count * WIDTH,
            transcendentals=0,
        ),
    )(
        *[
            pltpu.with_memory_space_constraint(operand, pltpu.HBM)
            for operand in (
                queries,
                key_vectors,
                value_vectors,
                token_rows.reshape(token_count // WIDTH, WIDTH),
                weight_table.transpose(2, 1, 0),
            )
        ]
    )
    return pl.pallas_call(
        functools.partial(finish_kernel, sizes),
        out_shape=jax.ShapeDtypeStruct(queries.shape, jnp.bfloat16),
        in_specs=[vmem] * 4,
        out_specs=hbm,
        scratch_shapes=[
            pltpu.VMEM(wide, jnp.bfloat16),
            pltpu.SemaphoreType.DMA((head_count, 4)),
        ],
        compiler_params=pltpu.CompilerParams(vmem_limit_bytes=32 * 1024 * 1024),
        cost_estimate=pl.CostEstimate(
            flops=4 * token_count * head_count * WIDTH * WIDTH,
            bytes_accessed=2 * token_count * head_count * WIDTH,
            transcendentals=0,
        ),
    )(acc, q_v, remote, weights)


def solution(mesh):
    placed = (
        P(("groups", "ctx"), "head"),
        P(("groups", "ctx"), "head"),
        P(("groups", "ctx"), "head"),
        P(("groups", "ctx")),
        P(None, "head", None),
    )
    return jax.shard_map(
        body, mesh=mesh, in_specs=placed, out_specs=P(("groups", "ctx"), "head"), check_vma=False
    )
```

```python
import functools

import jax
import jax.numpy as jnp
from jax import lax
from jax.experimental import pallas as pl
from jax.experimental.pallas import tpu as pltpu
from jax.sharding import PartitionSpec as P

BLOCK = 256
HALF = 128
WIDTH = 128
NT = (((1,), (1,)), ((), ()))


def level_constant(level_id):
    return 1.0 if level_id == 0 else 2.0 ** (-(level_id - 1) / 2.0)


def round_up(size, unit):
    return (size + unit - 1) // unit * unit


def node_index(block_count, bit, group):
    start = sum(block_count >> (low + 1) for low in range(bit))
    return start + group


def pair_tile(weight_rows):
    source = lax.broadcasted_iota(jnp.int32, (8, HALF), 0)
    target = lax.broadcasted_iota(jnp.int32, (8, HALF), 1)
    near_target = target & 7
    near_xor = source ^ near_target
    near = jnp.where(near_xor >= 1, weight_rows[1], weight_rows[0])
    near = jnp.where(near_xor >= 2, weight_rows[2], near)
    near = jnp.where(near_xor >= 4, weight_rows[3], near)
    near = jnp.where(source <= near_target, near, 0.0)
    spans = [jnp.zeros((8, HALF), jnp.float32)]
    for level_id in (7, 6, 5, 4):
        wider = []
        for index, span in enumerate(spans):
            right = target >> (level_id - 1) == 2 * index + 1
            wider += [jnp.where(right, weight_rows[level_id], span), span]
        spans = wider
    return jnp.concatenate(
        [jnp.where(target >> 3 == row, near, span) for row, span in enumerate(spans)], axis=0
    )


def kernel(
    sizes,
    q_hbm,
    k_hbm,
    v_hbm,
    tok_hbm,
    tab_hbm,
    acc,
    q_v,
    remote,
    weights,
    k_v,
    v_v,
    vt_v,
    nodes,
    left,
    total,
    lift,
    landed,
    tok_ref,
    tab_ref,
    table_pad,
    load_sem,
    small_sem,
    send_sem,
    recv_sem,
):
    head_count, block_count, level_count, table_count, shards, device_bits = sizes
    block_bits = BLOCK.bit_length() - 1
    local_bits = block_count.bit_length() - 1
    padded = round_up(level_count, 8)
    me = lax.axis_index("ctx")

    def load(array_id, head_id):
        source = (k_hbm, v_hbm, q_hbm)[array_id]
        target = (k_v, v_v, q_v)[array_id]
        column = pl.multiple_of(head_id * WIDTH, WIDTH)
        return pltpu.make_async_copy(
            source.at[:, pl.ds(column, WIDTH)], target.at[head_id], load_sem.at[array_id, head_id]
        )

    tokens_in = pltpu.make_async_copy(tok_hbm, tok_ref, small_sem.at[0])
    table_in = pltpu.make_async_copy(tab_hbm, tab_ref, small_sem.at[1])
    tokens_in.start()
    table_in.start()
    for head_id in range(min(2, head_count)):
        load(0, head_id).start()
        load(1, head_id).start()

    if shards > 1:
        barrier = pltpu.get_barrier_semaphore()

        @pl.when(me > 0)
        def _():
            pl.semaphore_signal(
                barrier, inc=1, device_id={"ctx": me - 1}, device_id_type=pl.DeviceIdType.MESH
            )

    level_row = lax.broadcasted_iota(jnp.int32, (padded, WIDTH), 0)
    scale = jnp.zeros((padded, WIDTH), jnp.float32)
    for level_id in range(level_count):
        scale = jnp.where(level_row == level_id, level_constant(level_id), scale)
    table_rows = []
    table_pad[...] = jnp.zeros_like(table_pad)
    tokens_in.wait()
    table_in.wait()
    for head_id in range(head_count):
        table_pad[0:level_count, 0:table_count] = tab_ref[:, head_id, :]
        table_rows.append(table_pad[...] * scale)
    table_all = jnp.concatenate(table_rows, axis=0)
    high = table_all.astype(jnp.bfloat16)
    rest = table_all - high.astype(jnp.float32)
    middle = rest.astype(jnp.bfloat16)
    low = (rest - middle.astype(jnp.float32)).astype(jnp.bfloat16)
    split = jnp.concatenate([high, middle, low], axis=0)
    rows = head_count * padded

    def weigh(block):
        tokens = jnp.concatenate(
            [tok_ref[pl.ds(2 * block, 1), :], tok_ref[pl.ds(2 * block + 1, 1), :]], axis=1
        )
        picks = lax.broadcasted_iota(jnp.int32, (WIDTH, BLOCK), 0) == tokens
        one_hot = jnp.where(picks, 1.0, 0.0).astype(jnp.bfloat16)
        parts = jnp.dot(split, one_hot, preferred_element_type=jnp.float32)
        whole = parts[0:rows] + parts[rows : 2 * rows] + parts[2 * rows :]
        for head_id in range(head_count):
            weights[block, head_id] = whole[head_id * padded : (head_id + 1) * padded]

    def remote_copy(source, bit, head_id):
        return pltpu.make_async_remote_copy(
            src_ref=source,
            dst_ref=landed.at[bit, head_id],
            send_sem=send_sem.at[bit, head_id],
            recv_sem=recv_sem.at[bit, head_id],
            device_id={"ctx": me + 1},
            device_id_type=pl.DeviceIdType.MESH,
        )

    def has_bit(bit):
        return lax.rem(lax.div(me, 2**bit), 2) == 1

    def ends_span(bit):
        return lax.rem(me, 2**bit) == 2**bit - 1

    def is_source(bit):
        return jnp.logical_and(ends_span(bit), jnp.logical_not(has_bit(bit)))

    def is_relay(bit):
        return jnp.logical_and(has_bit(bit), jnp.logical_not(ends_span(bit)))

    if shards > 1:

        @pl.when(me < shards - 1)
        def _():
            pl.semaphore_wait(barrier, 1)

    def states(head_id, carry):
        load(0, head_id).wait()
        load(1, head_id).wait()

        @pl.when(head_id + 2 < head_count)
        def _():
            load(0, head_id + 2).start()
            load(1, head_id + 2).start()

        load(2, head_id).start()

        def turn(block):
            span = pl.ds(block * BLOCK, BLOCK)
            value_t = jnp.transpose(v_v[head_id, span, :])
            vt_v[head_id, :, span] = value_t
            return value_t

        value_next = turn(0)
        for block in range(block_count):
            span = pl.ds(block * BLOCK, BLOCK)
            value_t = value_next
            if block + 1 < block_count:
                value_next = turn(block + 1)
            if block % head_count == head_count - 1:
                weigh(head_id * (block_count // head_count) + block // head_count)
            state = jnp.dot(value_t, k_v[head_id, span, :], preferred_element_type=jnp.float32)
            bit = 0
            while block >> bit & 1:
                state = left[bit] + state
                bit += 1
            if bit < local_bits:
                left[bit] = state
                nodes[head_id, node_index(block_count, bit, block >> (bit + 1))] = state.astype(
                    jnp.bfloat16
                )
            else:
                total[head_id] = state
        for bit in range(device_bits):

            @pl.when(jnp.logical_not(has_bit(bit)))
            def _(bit=bit):
                landed[bit, head_id] = jnp.zeros((WIDTH, WIDTH), jnp.float32)

        if shards > 1:

            @pl.when(is_source(0))
            def _():
                remote_copy(total.at[head_id], 0, head_id).start()

        return carry

    lax.fori_loop(0, head_count, states, 0)

    def service(bit, head_id):
        @pl.when(jnp.logical_and(has_bit(bit), me < shards - 1))
        def _():
            remote_copy(total.at[head_id], bit, head_id).wait_recv()

        @pl.when(is_relay(bit))
        def _():
            remote_copy(landed.at[bit, head_id], bit, head_id).start()

        if bit + 1 < device_bits:

            @pl.when(jnp.logical_and(ends_span(bit + 1), me < shards - 1))
            def _():
                base = total[head_id] if bit == 0 else lift[bit - 1, head_id]
                lift[bit, head_id] = base + landed[bit, head_id]

            @pl.when(is_source(bit + 1))
            def _():
                remote_copy(lift.at[bit, head_id], bit + 1, head_id).start()

    segment = block_count // 4
    due = sorted(
        (1 + 5 * bit + 2 * head_id, bit, head_id)
        for bit in range(device_bits)
        for head_id in range(head_count)
    )

    def weight_row(block, head_id, level_id):
        return weights[block, head_id, level_id : level_id + 1, :]

    def inside(head_id, carry):
        load(2, head_id).wait()

        def levels_of(block):
            return [bit for bit in range(local_bits) if block >> bit & 1]

        def weigh_pairs(block):
            span = pl.ds(block * BLOCK, BLOCK)
            bits = levels_of(block)
            query = q_v[head_id, span, :]
            stack = [k_v[head_id, span, :]] + [
                nodes[head_id, node_index(block_count, bit, block >> (bit + 1))] for bit in bits
            ]
            product = lax.dot_general(
                jnp.concatenate(stack, axis=0), query, NT, preferred_element_type=jnp.float32
            )
            level_rows = [
                weight_row(block, head_id, level_id) for level_id in range(block_bits + 1)
            ]
            first = pair_tile([jnp.broadcast_to(row[:, :HALF], (8, HALF)) for row in level_rows])
            second = pair_tile([jnp.broadcast_to(row[:, HALF:], (8, HALF)) for row in level_rows])
            top = jnp.concatenate(
                [
                    (product[:HALF, :HALF] * first).astype(jnp.bfloat16),
                    (product[:HALF, HALF:] * level_rows[block_bits][:, HALF:]).astype(jnp.bfloat16),
                ],
                axis=1,
            )
            bottom = jnp.concatenate(
                [
                    jnp.zeros((HALF, HALF), jnp.bfloat16),
                    (product[HALF:BLOCK, HALF:] * second).astype(jnp.bfloat16),
                ],
                axis=1,
            )
            distant = None
            for place, bit in enumerate(bits):
                begin = BLOCK + place * WIDTH
                term = product[begin : begin + WIDTH] * weight_row(
                    block, head_id, block_bits + 1 + bit
                )
                distant = term if distant is None else distant + term
            return jnp.concatenate([top, bottom], axis=0), distant

        pairs_next = weigh_pairs(0)
        for block in range(block_count):
            if block % segment == 0:
                for point, bit, which in due:
                    if point % 4 == block // segment and point < 4 * head_count:

                        @pl.when(head_id == point // 4)
                        def _(bit=bit, which=which):
                            service(bit, which)

            weighted, distant = pairs_next
            if block + 1 < block_count:
                pairs_next = weigh_pairs(block + 1)
            result = jnp.dot(
                vt_v[head_id, :, pl.ds(block * BLOCK, BLOCK)],
                weighted,
                preferred_element_type=jnp.float32,
            )
            acc[head_id, block] = result if distant is None else result + distant
        return carry

    lax.fori_loop(0, head_count, inside, 0)
    for point, bit, head_id in due:
        if point >= 4 * head_count:
            service(bit, head_id)

    if shards > 1:

        @pl.when(me == shards - 1)
        def _():
            for bit in range(device_bits):
                for head_id in range(head_count):
                    remote_copy(total.at[head_id], bit, head_id).wait_recv()

    for bit in range(device_bits):
        for head_id in range(head_count):
            remote[head_id, bit * WIDTH : (bit + 1) * WIDTH, :] = landed[bit, head_id].astype(
                jnp.bfloat16
            )
    for bit in range(device_bits):

        @pl.when(jnp.logical_or(is_source(bit), is_relay(bit)))
        def _(bit=bit):
            for head_id in range(head_count):
                remote_copy(total.at[head_id], bit, head_id).wait_send()


def finish_kernel(sizes, acc, q_v, remote, weights, out_hbm, out_v, out_sem):
    head_count, block_count, level_count, table_count, shards, device_bits = sizes
    first_level = BLOCK.bit_length() + block_count.bit_length() - 1
    padded = round_up(level_count, 8)
    chunk = max(1, block_count // 4)

    def write(head_id, part):
        column = pl.multiple_of(head_id * WIDTH, WIDTH)
        lines = pl.ds(part * chunk * BLOCK, chunk * BLOCK)
        return pltpu.make_async_copy(
            out_v.at[head_id, lines, :],
            out_hbm.at[lines, pl.ds(column, WIDTH)],
            out_sem.at[head_id, part],
        )

    def finish(head_id, carry):
        def add_up(block):
            result = acc[head_id, block]
            if device_bits:
                product = lax.dot_general(
                    remote[head_id],
                    q_v[head_id, pl.ds(block * BLOCK, BLOCK), :],
                    NT,
                    preferred_element_type=jnp.float32,
                )
            for bit in range(device_bits):
                row = weights[block, head_id, first_level + bit : first_level + bit + 1, :]
                result = result + product[bit * WIDTH : (bit + 1) * WIDTH] * row
            return result.astype(jnp.bfloat16)

        result_next = add_up(0)
        for block in range(block_count):
            result = result_next
            if block + 1 < block_count:
                result_next = add_up(block + 1)
            out_v[head_id, pl.ds(block * BLOCK, BLOCK), :] = jnp.transpose(result)
            if block % chunk == chunk - 1:
                write(head_id, block // chunk).start()
        return carry

    lax.fori_loop(0, head_count, finish, 0)
    for head_id in range(head_count):
        for part in range(block_count // chunk):
            write(head_id, part).wait()


def body(queries, key_vectors, value_vectors, token_rows, weight_table):
    table_count, head_count, level_count = weight_table.shape
    token_count = queries.shape[0]
    block_count = token_count // BLOCK
    shards = lax.axis_size("ctx")
    device_bits = shards.bit_length() - 1
    padded = round_up(level_count, 8)
    slots = max(1, device_bits)
    sizes = (head_count, block_count, level_count, table_count, shards, device_bits)
    hbm = pl.BlockSpec(memory_space=pltpu.HBM)
    vmem = pl.BlockSpec(memory_space=pltpu.VMEM)
    wide = (head_count, token_count, WIDTH)
    state = (WIDTH, WIDTH)
    acc, q_v, remote, weights = pl.pallas_call(
        functools.partial(kernel, sizes),
        out_shape=[
            jax.ShapeDtypeStruct((head_count, block_count, WIDTH, BLOCK), jnp.float32),
            jax.ShapeDtypeStruct(wide, jnp.bfloat16),
            jax.ShapeDtypeStruct((head_count, slots * WIDTH, WIDTH), jnp.bfloat16),
            jax.ShapeDtypeStruct((block_count, head_count, padded, BLOCK), jnp.float32),
        ],
        in_specs=[hbm] * 5,
        out_specs=[vmem] * 4,
        scratch_shapes=[
            pltpu.VMEM(wide, jnp.bfloat16),
            pltpu.VMEM(wide, jnp.bfloat16),
            pltpu.VMEM((head_count, WIDTH, token_count), jnp.bfloat16),
            pltpu.VMEM((head_count, max(1, block_count - 1)) + state, jnp.bfloat16),
            pltpu.VMEM((max(1, block_count.bit_length() - 1),) + state, jnp.float32),
            pltpu.VMEM((head_count,) + state, jnp.float32),
            pltpu.VMEM((slots, head_count) + state, jnp.float32),
            pltpu.VMEM((slots, head_count) + state, jnp.float32),
            pltpu.VMEM((token_count // WIDTH, WIDTH), jnp.int32),
            pltpu.VMEM((level_count, head_count, table_count), jnp.float32),
            pltpu.VMEM((padded, WIDTH), jnp.float32),
            pltpu.SemaphoreType.DMA((3, head_count)),
            pltpu.SemaphoreType.DMA((2,)),
            pltpu.SemaphoreType.DMA((slots, head_count)),
            pltpu.SemaphoreType.DMA((slots, head_count)),
        ],
        compiler_params=pltpu.CompilerParams(
            collective_id=0, has_side_effects=True, vmem_limit_bytes=32 * 1024 * 1024
        ),
        cost_estimate=pl.CostEstimate(
            flops=10 * token_count * head_count * WIDTH * BLOCK,
            bytes_accessed=6 * token_count * head_count * WIDTH,
            transcendentals=0,
        ),
    )(
        *[
            pltpu.with_memory_space_constraint(operand, pltpu.HBM)
            for operand in (
                queries,
                key_vectors,
                value_vectors,
                token_rows.reshape(token_count // WIDTH, WIDTH),
                weight_table.transpose(2, 1, 0),
            )
        ]
    )
    return pl.pallas_call(
        functools.partial(finish_kernel, sizes),
        out_shape=jax.ShapeDtypeStruct(queries.shape, jnp.bfloat16),
        in_specs=[vmem] * 4,
        out_specs=hbm,
        scratch_shapes=[
            pltpu.VMEM(wide, jnp.bfloat16),
            pltpu.SemaphoreType.DMA((head_count, 4)),
        ],
        compiler_params=pltpu.CompilerParams(vmem_limit_bytes=32 * 1024 * 1024),
        cost_estimate=pl.CostEstimate(
            flops=4 * token_count * head_count * WIDTH * WIDTH,
            bytes_accessed=2 * token_count * head_count * WIDTH,
            transcendentals=0,
        ),
    )(acc, q_v, remote, weights)


def solution(mesh):
    placed = (
        P(("groups", "ctx"), "head"),
        P(("groups", "ctx"), "head"),
        P(("groups", "ctx"), "head"),
        P(("groups", "ctx")),
        P(None, "head", None),
    )
    return jax.shard_map(
        body, mesh=mesh, in_specs=placed, out_specs=P(("groups", "ctx"), "head"), check_vma=False
    )
```

```python
import functools

import jax
import jax.numpy as jnp
from jax import lax
from jax.experimental import pallas as pl
from jax.experimental.pallas import tpu as pltpu
from jax.sharding import PartitionSpec as P

BLOCK = 256
HALF = 128
WIDTH = 128
NT = (((1,), (1,)), ((), ()))


def level_constant(level_id):
    return 1.0 if level_id == 0 else 2.0 ** (-(level_id - 1) / 2.0)


def round_up(size, unit):
    return (size + unit - 1) // unit * unit


def node_index(block_count, bit, group):
    start = sum(block_count >> (low + 1) for low in range(bit))
    return start + group


def pair_tile(weight_rows):
    source = lax.broadcasted_iota(jnp.int32, (8, HALF), 0)
    target = lax.broadcasted_iota(jnp.int32, (8, HALF), 1)
    near_target = target & 7
    near_xor = source ^ near_target
    near = jnp.where(near_xor >= 1, weight_rows[1], weight_rows[0])
    near = jnp.where(near_xor >= 2, weight_rows[2], near)
    near = jnp.where(near_xor >= 4, weight_rows[3], near)
    near = jnp.where(source <= near_target, near, 0.0)
    spans = [jnp.zeros((8, HALF), jnp.float32)]
    for level_id in (7, 6, 5, 4):
        wider = []
        for index, span in enumerate(spans):
            right = target >> (level_id - 1) == 2 * index + 1
            wider += [jnp.where(right, weight_rows[level_id], span), span]
        spans = wider
    return jnp.concatenate(
        [jnp.where(target >> 3 == row, near, span) for row, span in enumerate(spans)], axis=0
    )


def kernel(
    sizes,
    q_hbm,
    k_hbm,
    v_hbm,
    tok_hbm,
    tab_hbm,
    acc,
    q_v,
    remote,
    weights,
    k_v,
    v_v,
    vt_v,
    nodes,
    left,
    total,
    lift,
    landed,
    tok_ref,
    tab_ref,
    table_pad,
    load_sem,
    small_sem,
    send_sem,
    recv_sem,
):
    head_count, block_count, level_count, table_count, shards, device_bits = sizes
    block_bits = BLOCK.bit_length() - 1
    local_bits = block_count.bit_length() - 1
    padded = round_up(level_count, 8)
    me = lax.axis_index("ctx")

    half_rows = block_count // 2 * BLOCK

    def load(array_id, head_id, part):
        source = (k_hbm, v_hbm, q_hbm)[array_id]
        target = (k_v, v_v, q_v)[array_id]
        column = pl.multiple_of(head_id * WIDTH, WIDTH)
        return pltpu.make_async_copy(
            source.at[pl.ds(part * half_rows, half_rows), pl.ds(column, WIDTH)],
            target.at[head_id, pl.ds(part * half_rows, half_rows), :],
            load_sem.at[array_id, head_id, part],
        )

    tokens_in = pltpu.make_async_copy(tok_hbm, tok_ref, small_sem.at[0])
    table_in = pltpu.make_async_copy(tab_hbm, tab_ref, small_sem.at[1])
    tokens_in.start()
    table_in.start()
    for head_id in range(min(2, head_count)):
        for part in range(2):
            load(1, head_id, part).start()
            load(0, head_id, part).start()

    if shards > 1:
        barrier = pltpu.get_barrier_semaphore()

        @pl.when(me > 0)
        def _():
            pl.semaphore_signal(
                barrier, inc=1, device_id={"ctx": me - 1}, device_id_type=pl.DeviceIdType.MESH
            )

    level_row = lax.broadcasted_iota(jnp.int32, (padded, WIDTH), 0)
    scale = jnp.zeros((padded, WIDTH), jnp.float32)
    for level_id in range(level_count):
        scale = jnp.where(level_row == level_id, level_constant(level_id), scale)
    table_rows = []
    table_pad[...] = jnp.zeros_like(table_pad)
    tokens_in.wait()
    table_in.wait()
    for head_id in range(head_count):
        table_pad[0:level_count, 0:table_count] = tab_ref[:, head_id, :]
        table_rows.append(table_pad[...] * scale)
    table_all = jnp.concatenate(table_rows, axis=0)
    high = table_all.astype(jnp.bfloat16)
    rest = table_all - high.astype(jnp.float32)
    middle = rest.astype(jnp.bfloat16)
    low = (rest - middle.astype(jnp.float32)).astype(jnp.bfloat16)
    split = jnp.concatenate([high, middle, low], axis=0)
    rows = head_count * padded

    def weigh(block):
        tokens = jnp.concatenate(
            [tok_ref[pl.ds(2 * block, 1), :], tok_ref[pl.ds(2 * block + 1, 1), :]], axis=1
        )
        picks = lax.broadcasted_iota(jnp.int32, (WIDTH, BLOCK), 0) == tokens
        one_hot = jnp.where(picks, 1.0, 0.0).astype(jnp.bfloat16)
        parts = jnp.dot(split, one_hot, preferred_element_type=jnp.float32)
        whole = parts[0:rows] + parts[rows : 2 * rows] + parts[2 * rows :]
        for head_id in range(head_count):
            weights[block, head_id] = whole[head_id * padded : (head_id + 1) * padded]

    def remote_copy(source, bit, head_id):
        return pltpu.make_async_remote_copy(
            src_ref=source,
            dst_ref=landed.at[bit, head_id],
            send_sem=send_sem.at[bit, head_id],
            recv_sem=recv_sem.at[bit, head_id],
            device_id={"ctx": me + 1},
            device_id_type=pl.DeviceIdType.MESH,
        )

    def has_bit(bit):
        return lax.rem(lax.div(me, 2**bit), 2) == 1

    def ends_span(bit):
        return lax.rem(me, 2**bit) == 2**bit - 1

    def is_source(bit):
        return jnp.logical_and(ends_span(bit), jnp.logical_not(has_bit(bit)))

    def is_relay(bit):
        return jnp.logical_and(has_bit(bit), jnp.logical_not(ends_span(bit)))

    def states(head_id, carry):
        @pl.when(head_id + 2 < head_count)
        def _():
            for part in range(2):
                load(1, head_id + 2, part).start()
                load(0, head_id + 2, part).start()

        for part in range(2):
            load(2, head_id, part).start()

        def turn(block):
            if block % (block_count // 2) == 0:
                load(1, head_id, 2 * block // block_count).wait()
                load(0, head_id, 2 * block // block_count).wait()
            span = pl.ds(block * BLOCK, BLOCK)
            value_t = jnp.transpose(v_v[head_id, span, :])
            vt_v[head_id, :, span] = value_t
            return value_t

        value_next = turn(0)
        for block in range(block_count):
            span = pl.ds(block * BLOCK, BLOCK)
            value_t = value_next
            if block + 1 < block_count:
                value_next = turn(block + 1)
            if block % head_count == head_count - 1:
                weigh(head_id * (block_count // head_count) + block // head_count)
            state = jnp.dot(value_t, k_v[head_id, span, :], preferred_element_type=jnp.float32)
            bit = 0
            while block >> bit & 1:
                state = left[bit] + state
                bit += 1
            if bit < local_bits:
                left[bit] = state
                nodes[head_id, node_index(block_count, bit, block >> (bit + 1))] = state.astype(
                    jnp.bfloat16
                )
            else:
                total[head_id] = state
        for bit in range(device_bits):

            @pl.when(jnp.logical_not(has_bit(bit)))
            def _(bit=bit):
                landed[bit, head_id] = jnp.zeros((WIDTH, WIDTH), jnp.float32)

        if shards > 1:

            @pl.when(jnp.logical_and(head_id == 0, me < shards - 1))
            def _():
                pl.semaphore_wait(barrier, 1)

            @pl.when(is_source(0))
            def _():
                remote_copy(total.at[head_id], 0, head_id).start()

        return carry

    lax.fori_loop(0, head_count, states, 0)

    def service(bit, head_id):
        @pl.when(jnp.logical_and(has_bit(bit), me < shards - 1))
        def _():
            remote_copy(total.at[head_id], bit, head_id).wait_recv()

        @pl.when(is_relay(bit))
        def _():
            remote_copy(landed.at[bit, head_id], bit, head_id).start()

        if bit + 1 < device_bits:

            @pl.when(jnp.logical_and(ends_span(bit + 1), me < shards - 1))
            def _():
                base = total[head_id] if bit == 0 else lift[bit - 1, head_id]
                lift[bit, head_id] = base + landed[bit, head_id]

            @pl.when(is_source(bit + 1))
            def _():
                remote_copy(lift.at[bit, head_id], bit + 1, head_id).start()

    segment = block_count // 4
    due = sorted(
        (1 + 5 * bit + 2 * head_id, bit, head_id)
        for bit in range(device_bits)
        for head_id in range(head_count)
    )

    def weight_row(block, head_id, level_id):
        return weights[block, head_id, level_id : level_id + 1, :]

    def inside(head_id, carry):
        for part in range(2):
            load(2, head_id, part).wait()

        def levels_of(block):
            return [bit for bit in range(local_bits) if block >> bit & 1]

        def weigh_pairs(block):
            span = pl.ds(block * BLOCK, BLOCK)
            bits = levels_of(block)
            query = q_v[head_id, span, :]
            stack = [k_v[head_id, span, :]] + [
                nodes[head_id, node_index(block_count, bit, block >> (bit + 1))] for bit in bits
            ]
            product = lax.dot_general(
                jnp.concatenate(stack, axis=0), query, NT, preferred_element_type=jnp.float32
            )
            level_rows = [
                weight_row(block, head_id, level_id) for level_id in range(block_bits + 1)
            ]
            first = pair_tile([jnp.broadcast_to(row[:, :HALF], (8, HALF)) for row in level_rows])
            second = pair_tile([jnp.broadcast_to(row[:, HALF:], (8, HALF)) for row in level_rows])
            top = jnp.concatenate(
                [
                    (product[:HALF, :HALF] * first).astype(jnp.bfloat16),
                    (product[:HALF, HALF:] * level_rows[block_bits][:, HALF:]).astype(jnp.bfloat16),
                ],
                axis=1,
            )
            bottom = jnp.concatenate(
                [
                    jnp.zeros((HALF, HALF), jnp.bfloat16),
                    (product[HALF:BLOCK, HALF:] * second).astype(jnp.bfloat16),
                ],
                axis=1,
            )
            distant = None
            for place, bit in enumerate(bits):
                begin = BLOCK + place * WIDTH
                term = product[begin : begin + WIDTH] * weight_row(
                    block, head_id, block_bits + 1 + bit
                )
                distant = term if distant is None else distant + term
            return jnp.concatenate([top, bottom], axis=0), distant

        pairs_next = weigh_pairs(0)
        for block in range(block_count):
            if block % segment == 0:
                for point, bit, which in due:
                    if point % 4 == block // segment and point < 4 * head_count:

                        @pl.when(head_id == point // 4)
                        def _(bit=bit, which=which):
                            service(bit, which)

            weighted, distant = pairs_next
            if block + 1 < block_count:
                pairs_next = weigh_pairs(block + 1)
            result = jnp.dot(
                vt_v[head_id, :, pl.ds(block * BLOCK, BLOCK)],
                weighted,
                preferred_element_type=jnp.float32,
            )
            acc[head_id, block] = result if distant is None else result + distant
        return carry

    lax.fori_loop(0, head_count, inside, 0)
    for point, bit, head_id in due:
        if point >= 4 * head_count:
            service(bit, head_id)

    if shards > 1:

        @pl.when(me == shards - 1)
        def _():
            for bit in range(device_bits):
                for head_id in range(head_count):
                    remote_copy(total.at[head_id], bit, head_id).wait_recv()

    for bit in range(device_bits):
        for head_id in range(head_count):
            remote[head_id, bit * WIDTH : (bit + 1) * WIDTH, :] = landed[bit, head_id].astype(
                jnp.bfloat16
            )
    for bit in range(device_bits):

        @pl.when(jnp.logical_or(is_source(bit), is_relay(bit)))
        def _(bit=bit):
            for head_id in range(head_count):
                remote_copy(total.at[head_id], bit, head_id).wait_send()


def finish_kernel(sizes, acc, q_v, remote, weights, out_hbm, out_v, out_sem):
    head_count, block_count, level_count, table_count, shards, device_bits = sizes
    first_level = BLOCK.bit_length() + block_count.bit_length() - 1
    padded = round_up(level_count, 8)
    chunk = max(1, block_count // 4)

    def write(head_id, part):
        column = pl.multiple_of(head_id * WIDTH, WIDTH)
        lines = pl.ds(part * chunk * BLOCK, chunk * BLOCK)
        return pltpu.make_async_copy(
            out_v.at[head_id, lines, :],
            out_hbm.at[lines, pl.ds(column, WIDTH)],
            out_sem.at[head_id, part],
        )

    def finish(head_id, carry):
        def add_up(block):
            result = acc[head_id, block]
            if device_bits:
                product = lax.dot_general(
                    remote[head_id],
                    q_v[head_id, pl.ds(block * BLOCK, BLOCK), :],
                    NT,
                    preferred_element_type=jnp.float32,
                )
            for bit in range(device_bits):
                row = weights[block, head_id, first_level + bit : first_level + bit + 1, :]
                result = result + product[bit * WIDTH : (bit + 1) * WIDTH] * row
            return result.astype(jnp.bfloat16)

        result_next = add_up(0)
        for block in range(block_count):
            result = result_next
            if block + 1 < block_count:
                result_next = add_up(block + 1)
            out_v[head_id, pl.ds(block * BLOCK, BLOCK), :] = jnp.transpose(result)
            if block % chunk == chunk - 1:
                write(head_id, block // chunk).start()
        return carry

    lax.fori_loop(0, head_count, finish, 0)
    for head_id in range(head_count):
        for part in range(block_count // chunk):
            write(head_id, part).wait()


def body(queries, key_vectors, value_vectors, token_rows, weight_table):
    table_count, head_count, level_count = weight_table.shape
    token_count = queries.shape[0]
    block_count = token_count // BLOCK
    shards = lax.axis_size("ctx")
    device_bits = shards.bit_length() - 1
    padded = round_up(level_count, 8)
    slots = max(1, device_bits)
    sizes = (head_count, block_count, level_count, table_count, shards, device_bits)
    hbm = pl.BlockSpec(memory_space=pltpu.HBM)
    vmem = pl.BlockSpec(memory_space=pltpu.VMEM)
    wide = (head_count, token_count, WIDTH)
    state = (WIDTH, WIDTH)
    acc, q_v, remote, weights = pl.pallas_call(
        functools.partial(kernel, sizes),
        out_shape=[
            jax.ShapeDtypeStruct((head_count, block_count, WIDTH, BLOCK), jnp.float32),
            jax.ShapeDtypeStruct(wide, jnp.bfloat16),
            jax.ShapeDtypeStruct((head_count, slots * WIDTH, WIDTH), jnp.bfloat16),
            jax.ShapeDtypeStruct((block_count, head_count, padded, BLOCK), jnp.float32),
        ],
        in_specs=[hbm] * 5,
        out_specs=[vmem] * 4,
        scratch_shapes=[
            pltpu.VMEM(wide, jnp.bfloat16),
            pltpu.VMEM(wide, jnp.bfloat16),
            pltpu.VMEM((head_count, WIDTH, token_count), jnp.bfloat16),
            pltpu.VMEM((head_count, max(1, block_count - 1)) + state, jnp.bfloat16),
            pltpu.VMEM((max(1, block_count.bit_length() - 1),) + state, jnp.float32),
            pltpu.VMEM((head_count,) + state, jnp.float32),
            pltpu.VMEM((slots, head_count) + state, jnp.float32),
            pltpu.VMEM((slots, head_count) + state, jnp.float32),
            pltpu.VMEM((token_count // WIDTH, WIDTH), jnp.int32),
            pltpu.VMEM((level_count, head_count, table_count), jnp.float32),
            pltpu.VMEM((padded, WIDTH), jnp.float32),
            pltpu.SemaphoreType.DMA((3, head_count, 2)),
            pltpu.SemaphoreType.DMA((2,)),
            pltpu.SemaphoreType.DMA((slots, head_count)),
            pltpu.SemaphoreType.DMA((slots, head_count)),
        ],
        compiler_params=pltpu.CompilerParams(
            collective_id=0, has_side_effects=True, vmem_limit_bytes=32 * 1024 * 1024
        ),
        cost_estimate=pl.CostEstimate(
            flops=10 * token_count * head_count * WIDTH * BLOCK,
            bytes_accessed=6 * token_count * head_count * WIDTH,
            transcendentals=0,
        ),
    )(
        *[
            pltpu.with_memory_space_constraint(operand, pltpu.HBM)
            for operand in (
                queries,
                key_vectors,
                value_vectors,
                token_rows.reshape(token_count // WIDTH, WIDTH),
                weight_table.transpose(2, 1, 0),
            )
        ]
    )
    return pl.pallas_call(
        functools.partial(finish_kernel, sizes),
        out_shape=jax.ShapeDtypeStruct(queries.shape, jnp.bfloat16),
        in_specs=[vmem] * 4,
        out_specs=hbm,
        scratch_shapes=[
            pltpu.VMEM(wide, jnp.bfloat16),
            pltpu.SemaphoreType.DMA((head_count, 4)),
        ],
        compiler_params=pltpu.CompilerParams(vmem_limit_bytes=32 * 1024 * 1024),
        cost_estimate=pl.CostEstimate(
            flops=4 * token_count * head_count * WIDTH * WIDTH,
            bytes_accessed=2 * token_count * head_count * WIDTH,
            transcendentals=0,
        ),
    )(acc, q_v, remote, weights)


def solution(mesh):
    placed = (
        P(("groups", "ctx"), "head"),
        P(("groups", "ctx"), "head"),
        P(("groups", "ctx"), "head"),
        P(("groups", "ctx")),
        P(None, "head", None),
    )
    return jax.shard_map(
        body, mesh=mesh, in_specs=placed, out_specs=P(("groups", "ctx"), "head"), check_vma=False
    )
```

```python
import functools

import jax
import jax.numpy as jnp
from jax import lax
from jax.experimental import pallas as pl
from jax.experimental.pallas import tpu as pltpu
from jax.sharding import PartitionSpec as P

BLOCK = 256
HALF = 128
WIDTH = 128
NT = (((1,), (1,)), ((), ()))


def level_constant(level_id):
    return 1.0 if level_id == 0 else 2.0 ** (-(level_id - 1) / 2.0)


def round_up(size, unit):
    return (size + unit - 1) // unit * unit


def node_index(block_count, bit, group):
    start = sum(block_count >> (low + 1) for low in range(bit))
    return start + group


def pair_tile(weight_rows):
    source = lax.broadcasted_iota(jnp.int32, (8, HALF), 0)
    target = lax.broadcasted_iota(jnp.int32, (8, HALF), 1)
    near_target = target & 7
    near_xor = source ^ near_target
    near = jnp.where(near_xor >= 1, weight_rows[1], weight_rows[0])
    near = jnp.where(near_xor >= 2, weight_rows[2], near)
    near = jnp.where(near_xor >= 4, weight_rows[3], near)
    near = jnp.where(source <= near_target, near, 0.0)
    spans = [jnp.zeros((8, HALF), jnp.float32)]
    for level_id in (7, 6, 5, 4):
        wider = []
        for index, span in enumerate(spans):
            right = target >> (level_id - 1) == 2 * index + 1
            wider += [jnp.where(right, weight_rows[level_id], span), span]
        spans = wider
    return jnp.concatenate(
        [jnp.where(target >> 3 == row, near, span) for row, span in enumerate(spans)], axis=0
    )


def kernel(
    sizes,
    q_hbm,
    k_hbm,
    v_hbm,
    tok_hbm,
    tab_hbm,
    acc,
    q_v,
    remote,
    weights,
    k_v,
    v_v,
    vt_v,
    nodes,
    left,
    total,
    lift,
    landed,
    tok_ref,
    tab_ref,
    table_pad,
    load_sem,
    small_sem,
    send_sem,
    recv_sem,
):
    head_count, block_count, level_count, table_count, shards, device_bits = sizes
    block_bits = BLOCK.bit_length() - 1
    local_bits = block_count.bit_length() - 1
    padded = round_up(level_count, 8)
    me = lax.axis_index("ctx")

    half_rows = block_count * BLOCK

    def load(array_id, head_id, part):
        source = (k_hbm, v_hbm, q_hbm)[array_id]
        target = (k_v, v_v, q_v)[array_id]
        column = pl.multiple_of(head_id * WIDTH, WIDTH)
        return pltpu.make_async_copy(
            source.at[pl.ds(part * half_rows, half_rows), pl.ds(column, WIDTH)],
            target.at[head_id, pl.ds(part * half_rows, half_rows), :],
            load_sem.at[array_id, head_id, part],
        )

    tokens_in = pltpu.make_async_copy(tok_hbm, tok_ref, small_sem.at[0])
    table_in = pltpu.make_async_copy(tab_hbm, tab_ref, small_sem.at[1])
    tokens_in.start()
    table_in.start()
    for head_id in range(min(2, head_count)):
        for part in range(1):
            load(1, head_id, part).start()
            load(0, head_id, part).start()

    if shards > 1:
        barrier = pltpu.get_barrier_semaphore()

        @pl.when(me > 0)
        def _():
            pl.semaphore_signal(
                barrier, inc=1, device_id={"ctx": me - 1}, device_id_type=pl.DeviceIdType.MESH
            )

    level_row = lax.broadcasted_iota(jnp.int32, (padded, WIDTH), 0)
    scale = jnp.zeros((padded, WIDTH), jnp.float32)
    for level_id in range(level_count):
        scale = jnp.where(level_row == level_id, level_constant(level_id), scale)
    table_rows = []
    table_pad[...] = jnp.zeros_like(table_pad)
    tokens_in.wait()
    table_in.wait()
    for head_id in range(head_count):
        table_pad[0:level_count, 0:table_count] = tab_ref[:, head_id, :]
        table_rows.append(table_pad[...] * scale)
    table_all = jnp.concatenate(table_rows, axis=0)
    high = table_all.astype(jnp.bfloat16)
    rest = table_all - high.astype(jnp.float32)
    middle = rest.astype(jnp.bfloat16)
    low = (rest - middle.astype(jnp.float32)).astype(jnp.bfloat16)
    split = jnp.concatenate([high, middle, low], axis=0)
    rows = head_count * padded

    def weigh(block):
        tokens = jnp.concatenate(
            [tok_ref[pl.ds(2 * block, 1), :], tok_ref[pl.ds(2 * block + 1, 1), :]], axis=1
        )
        picks = lax.broadcasted_iota(jnp.int32, (WIDTH, BLOCK), 0) == tokens
        one_hot = jnp.where(picks, 1.0, 0.0).astype(jnp.bfloat16)
        parts = jnp.dot(split, one_hot, preferred_element_type=jnp.float32)
        whole = parts[0:rows] + parts[rows : 2 * rows] + parts[2 * rows :]
        for head_id in range(head_count):
            weights[block, head_id] = whole[head_id * padded : (head_id + 1) * padded]

    def remote_copy(source, bit, head_id):
        return pltpu.make_async_remote_copy(
            src_ref=source,
            dst_ref=landed.at[bit, head_id],
            send_sem=send_sem.at[bit, head_id],
            recv_sem=recv_sem.at[bit, head_id],
            device_id={"ctx": me + 1},
            device_id_type=pl.DeviceIdType.MESH,
        )

    def has_bit(bit):
        return lax.rem(lax.div(me, 2**bit), 2) == 1

    def ends_span(bit):
        return lax.rem(me, 2**bit) == 2**bit - 1

    def is_source(bit):
        return jnp.logical_and(ends_span(bit), jnp.logical_not(has_bit(bit)))

    def is_relay(bit):
        return jnp.logical_and(has_bit(bit), jnp.logical_not(ends_span(bit)))

    def states(head_id, carry):
        @pl.when(head_id + 2 < head_count)
        def _():
            for part in range(1):
                load(1, head_id + 2, part).start()
                load(0, head_id + 2, part).start()

        for part in range(1):
            load(2, head_id, part).start()

        def turn(block):
            if block == 0:
                load(1, head_id, 0).wait()
                load(0, head_id, 0).wait()
            span = pl.ds(block * BLOCK, BLOCK)
            value_t = jnp.transpose(v_v[head_id, span, :])
            vt_v[head_id, :, span] = value_t
            return value_t

        value_next = turn(0)
        for block in range(block_count):
            span = pl.ds(block * BLOCK, BLOCK)
            value_t = value_next
            if block + 1 < block_count:
                value_next = turn(block + 1)
            if block % head_count == head_count - 1:
                weigh(head_id * (block_count // head_count) + block // head_count)
            state = jnp.dot(value_t, k_v[head_id, span, :], preferred_element_type=jnp.float32)
            bit = 0
            while block >> bit & 1:
                state = left[bit] + state
                bit += 1
            if bit < local_bits:
                left[bit] = state
                nodes[head_id, node_index(block_count, bit, block >> (bit + 1))] = state.astype(
                    jnp.bfloat16
                )
            else:
                total[head_id] = state
        for bit in range(device_bits):

            @pl.when(jnp.logical_not(has_bit(bit)))
            def _(bit=bit):
                landed[bit, head_id] = jnp.zeros((WIDTH, WIDTH), jnp.float32)

        if shards > 1:

            @pl.when(jnp.logical_and(head_id == 0, me < shards - 1))
            def _():
                pl.semaphore_wait(barrier, 1)

            @pl.when(is_source(0))
            def _():
                remote_copy(total.at[head_id], 0, head_id).start()

        return carry

    lax.fori_loop(0, head_count, states, 0)

    def service(bit, head_id):
        @pl.when(jnp.logical_and(has_bit(bit), me < shards - 1))
        def _():
            remote_copy(total.at[head_id], bit, head_id).wait_recv()

        @pl.when(is_relay(bit))
        def _():
            remote_copy(landed.at[bit, head_id], bit, head_id).start()

        if bit + 1 < device_bits:

            @pl.when(jnp.logical_and(ends_span(bit + 1), me < shards - 1))
            def _():
                base = total[head_id] if bit == 0 else lift[bit - 1, head_id]
                lift[bit, head_id] = base + landed[bit, head_id]

            @pl.when(is_source(bit + 1))
            def _():
                remote_copy(lift.at[bit, head_id], bit + 1, head_id).start()

    segment = block_count // 2
    due = sorted(
        (1 + 2 * bit + head_id, bit, head_id)
        for bit in range(device_bits)
        for head_id in range(head_count)
    )

    def weight_row(block, head_id, level_id):
        return weights[block, head_id, level_id : level_id + 1, :]

    def inside(head_id, carry):
        for part in range(1):
            load(2, head_id, part).wait()

        def levels_of(block):
            return [bit for bit in range(local_bits) if block >> bit & 1]

        def weigh_pairs(block):
            span = pl.ds(block * BLOCK, BLOCK)
            bits = levels_of(block)
            query = q_v[head_id, span, :]
            stack = [k_v[head_id, span, :]] + [
                nodes[head_id, node_index(block_count, bit, block >> (bit + 1))] for bit in bits
            ]
            product = lax.dot_general(
                jnp.concatenate(stack, axis=0), query, NT, preferred_element_type=jnp.float32
            )
            level_rows = [
                weight_row(block, head_id, level_id) for level_id in range(block_bits + 1)
            ]
            first = pair_tile([jnp.broadcast_to(row[:, :HALF], (8, HALF)) for row in level_rows])
            second = pair_tile([jnp.broadcast_to(row[:, HALF:], (8, HALF)) for row in level_rows])
            top = jnp.concatenate(
                [
                    (product[:HALF, :HALF] * first).astype(jnp.bfloat16),
                    (product[:HALF, HALF:] * level_rows[block_bits][:, HALF:]).astype(jnp.bfloat16),
                ],
                axis=1,
            )
            bottom = jnp.concatenate(
                [
                    jnp.zeros((HALF, HALF), jnp.bfloat16),
                    (product[HALF:BLOCK, HALF:] * second).astype(jnp.bfloat16),
                ],
                axis=1,
            )
            distant = None
            for place, bit in enumerate(bits):
                begin = BLOCK + place * WIDTH
                term = product[begin : begin + WIDTH] * weight_row(
                    block, head_id, block_bits + 1 + bit
                )
                distant = term if distant is None else distant + term
            return jnp.concatenate([top, bottom], axis=0), distant

        def pass_on(half):
            for point, bit, which in due:
                if point % 2 == half and point < 2 * head_count:

                    @pl.when(head_id == point // 2)
                    def _(bit=bit, which=which):
                        service(bit, which)

        pass_on(0)
        pairs_next = weigh_pairs(0)
        for block in range(block_count):
            if block == segment:
                pass_on(1)
            weighted, distant = pairs_next
            if block + 1 < block_count:
                pairs_next = weigh_pairs(block + 1)
            result = jnp.dot(
                vt_v[head_id, :, pl.ds(block * BLOCK, BLOCK)],
                weighted,
                preferred_element_type=jnp.float32,
            )
            acc[head_id, block] = result if distant is None else result + distant
        return carry

    lax.fori_loop(0, head_count, inside, 0)
    for point, bit, head_id in due:
        if point >= 2 * head_count:
            service(bit, head_id)

    if shards > 1:

        @pl.when(me == shards - 1)
        def _():
            for bit in range(device_bits):
                for head_id in range(head_count):
                    remote_copy(total.at[head_id], bit, head_id).wait_recv()

    for bit in range(device_bits):
        for head_id in range(head_count):
            remote[head_id, bit * WIDTH : (bit + 1) * WIDTH, :] = landed[bit, head_id].astype(
                jnp.bfloat16
            )
    for bit in range(device_bits):

        @pl.when(jnp.logical_or(is_source(bit), is_relay(bit)))
        def _(bit=bit):
            for head_id in range(head_count):
                remote_copy(total.at[head_id], bit, head_id).wait_send()


def finish_kernel(sizes, acc, q_v, remote, weights, out_hbm, out_v, out_sem):
    head_count, block_count, level_count, table_count, shards, device_bits = sizes
    first_level = BLOCK.bit_length() + block_count.bit_length() - 1
    padded = round_up(level_count, 8)
    chunk = max(1, block_count // 4)

    def write(head_id, part):
        column = pl.multiple_of(head_id * WIDTH, WIDTH)
        lines = pl.ds(part * chunk * BLOCK, chunk * BLOCK)
        return pltpu.make_async_copy(
            out_v.at[head_id, lines, :],
            out_hbm.at[lines, pl.ds(column, WIDTH)],
            out_sem.at[head_id, part],
        )

    def finish(head_id, carry):
        def add_up(block):
            result = acc[head_id, block]
            if device_bits:
                product = lax.dot_general(
                    remote[head_id],
                    q_v[head_id, pl.ds(block * BLOCK, BLOCK), :],
                    NT,
                    preferred_element_type=jnp.float32,
                )
            for bit in range(device_bits):
                row = weights[block, head_id, first_level + bit : first_level + bit + 1, :]
                result = result + product[bit * WIDTH : (bit + 1) * WIDTH] * row
            return result.astype(jnp.bfloat16)

        result_next = add_up(0)
        for block in range(block_count):
            result = result_next
            if block + 1 < block_count:
                result_next = add_up(block + 1)
            out_v[head_id, pl.ds(block * BLOCK, BLOCK), :] = jnp.transpose(result)
            if block % chunk == chunk - 1:
                write(head_id, block // chunk).start()
        return carry

    lax.fori_loop(0, head_count, finish, 0)
    for head_id in range(head_count):
        for part in range(block_count // chunk):
            write(head_id, part).wait()


def body(queries, key_vectors, value_vectors, token_rows, weight_table):
    table_count, head_count, level_count = weight_table.shape
    token_count = queries.shape[0]
    block_count = token_count // BLOCK
    shards = lax.axis_size("ctx")
    device_bits = shards.bit_length() - 1
    padded = round_up(level_count, 8)
    slots = max(1, device_bits)
    sizes = (head_count, block_count, level_count, table_count, shards, device_bits)
    hbm = pl.BlockSpec(memory_space=pltpu.HBM)
    vmem = pl.BlockSpec(memory_space=pltpu.VMEM)
    wide = (head_count, token_count, WIDTH)
    state = (WIDTH, WIDTH)
    acc, q_v, remote, weights = pl.pallas_call(
        functools.partial(kernel, sizes),
        out_shape=[
            jax.ShapeDtypeStruct((head_count, block_count, WIDTH, BLOCK), jnp.float32),
            jax.ShapeDtypeStruct(wide, jnp.bfloat16),
            jax.ShapeDtypeStruct((head_count, slots * WIDTH, WIDTH), jnp.bfloat16),
            jax.ShapeDtypeStruct((block_count, head_count, padded, BLOCK), jnp.float32),
        ],
        in_specs=[hbm] * 5,
        out_specs=[vmem] * 4,
        scratch_shapes=[
            pltpu.VMEM(wide, jnp.bfloat16),
            pltpu.VMEM(wide, jnp.bfloat16),
            pltpu.VMEM((head_count, WIDTH, token_count), jnp.bfloat16),
            pltpu.VMEM((head_count, max(1, block_count - 1)) + state, jnp.bfloat16),
            pltpu.VMEM((max(1, block_count.bit_length() - 1),) + state, jnp.float32),
            pltpu.VMEM((head_count,) + state, jnp.float32),
            pltpu.VMEM((slots, head_count) + state, jnp.float32),
            pltpu.VMEM((slots, head_count) + state, jnp.float32),
            pltpu.VMEM((token_count // WIDTH, WIDTH), jnp.int32),
            pltpu.VMEM((level_count, head_count, table_count), jnp.float32),
            pltpu.VMEM((padded, WIDTH), jnp.float32),
            pltpu.SemaphoreType.DMA((3, head_count, 1)),
            pltpu.SemaphoreType.DMA((2,)),
            pltpu.SemaphoreType.DMA((slots, head_count)),
            pltpu.SemaphoreType.DMA((slots, head_count)),
        ],
        compiler_params=pltpu.CompilerParams(
            collective_id=0, has_side_effects=True, vmem_limit_bytes=32 * 1024 * 1024
        ),
        cost_estimate=pl.CostEstimate(
            flops=10 * token_count * head_count * WIDTH * BLOCK,
            bytes_accessed=6 * token_count * head_count * WIDTH,
            transcendentals=0,
        ),
    )(
        *[
            pltpu.with_memory_space_constraint(operand, pltpu.HBM)
            for operand in (
                queries,
                key_vectors,
                value_vectors,
                token_rows.reshape(token_count // WIDTH, WIDTH),
                weight_table.transpose(2, 1, 0),
            )
        ]
    )
    return pl.pallas_call(
        functools.partial(finish_kernel, sizes),
        out_shape=jax.ShapeDtypeStruct(queries.shape, jnp.bfloat16),
        in_specs=[vmem] * 4,
        out_specs=hbm,
        scratch_shapes=[
            pltpu.VMEM(wide, jnp.bfloat16),
            pltpu.SemaphoreType.DMA((head_count, 4)),
        ],
        compiler_params=pltpu.CompilerParams(vmem_limit_bytes=32 * 1024 * 1024),
        cost_estimate=pl.CostEstimate(
            flops=4 * token_count * head_count * WIDTH * WIDTH,
            bytes_accessed=2 * token_count * head_count * WIDTH,
            transcendentals=0,
        ),
    )(acc, q_v, remote, weights)


def solution(mesh):
    placed = (
        P(("groups", "ctx"), "head"),
        P(("groups", "ctx"), "head"),
        P(("groups", "ctx"), "head"),
        P(("groups", "ctx")),
        P(None, "head", None),
    )
    return jax.shard_map(
        body, mesh=mesh, in_specs=placed, out_specs=P(("groups", "ctx"), "head"), check_vma=False
    )
```

```python
import functools

import jax
import jax.numpy as jnp
from jax import lax
from jax.experimental import pallas as pl
from jax.experimental.pallas import tpu as pltpu
from jax.sharding import PartitionSpec as P

BLOCK = 256
HALF = 128
WIDTH = 128
NT = (((1,), (1,)), ((), ()))


def level_constant(level_id):
    return 1.0 if level_id == 0 else 2.0 ** (-(level_id - 1) / 2.0)


def round_up(size, unit):
    return (size + unit - 1) // unit * unit


def node_index(block_count, bit, group):
    start = sum(block_count >> (low + 1) for low in range(bit))
    return start + group


def pair_tile(weight_rows):
    source = lax.broadcasted_iota(jnp.int32, (8, HALF), 0)
    target = lax.broadcasted_iota(jnp.int32, (8, HALF), 1)
    near_target = target & 7
    near_xor = source ^ near_target
    near = jnp.where(near_xor >= 1, weight_rows[1], weight_rows[0])
    near = jnp.where(near_xor >= 2, weight_rows[2], near)
    near = jnp.where(near_xor >= 4, weight_rows[3], near)
    near = jnp.where(source <= near_target, near, 0.0)
    spans = [jnp.zeros((8, HALF), jnp.float32)]
    for level_id in (7, 6, 5, 4):
        wider = []
        for index, span in enumerate(spans):
            right = target >> (level_id - 1) == 2 * index + 1
            wider += [jnp.where(right, weight_rows[level_id], span), span]
        spans = wider
    return jnp.concatenate(
        [jnp.where(target >> 3 == row, near, span) for row, span in enumerate(spans)], axis=0
    )


def kernel(
    sizes,
    q_hbm,
    k_hbm,
    v_hbm,
    tok_hbm,
    tab_hbm,
    acc,
    q_v,
    remote,
    weights,
    k_v,
    v_v,
    vt_v,
    nodes,
    left,
    total,
    lift,
    landed,
    tok_ref,
    tab_ref,
    table_pad,
    load_sem,
    small_sem,
    send_sem,
    recv_sem,
):
    head_count, block_count, level_count, table_count, shards, device_bits = sizes
    block_bits = BLOCK.bit_length() - 1
    local_bits = block_count.bit_length() - 1
    padded = round_up(level_count, 8)
    me = lax.axis_index("ctx")

    half_rows = block_count * BLOCK

    def load(array_id, head_id, part):
        source = (k_hbm, v_hbm, q_hbm)[array_id]
        target = (k_v, v_v, q_v)[array_id]
        column = pl.multiple_of(head_id * WIDTH, WIDTH)
        return pltpu.make_async_copy(
            source.at[pl.ds(part * half_rows, half_rows), pl.ds(column, WIDTH)],
            target.at[head_id, pl.ds(part * half_rows, half_rows), :],
            load_sem.at[array_id, head_id, part],
        )

    tokens_in = pltpu.make_async_copy(tok_hbm, tok_ref, small_sem.at[0])
    table_in = pltpu.make_async_copy(tab_hbm, tab_ref, small_sem.at[1])
    tokens_in.start()
    table_in.start()
    for head_id in range(min(2, head_count)):
        for part in range(1):
            load(1, head_id, part).start()
            load(0, head_id, part).start()

    if shards > 1:
        barrier = pltpu.get_barrier_semaphore()

        @pl.when(me > 0)
        def _():
            pl.semaphore_signal(
                barrier, inc=1, device_id={"ctx": me - 1}, device_id_type=pl.DeviceIdType.MESH
            )

    level_row = lax.broadcasted_iota(jnp.int32, (padded, WIDTH), 0)
    scale = jnp.zeros((padded, WIDTH), jnp.float32)
    for level_id in range(level_count):
        scale = jnp.where(level_row == level_id, level_constant(level_id), scale)
    table_rows = []
    table_pad[...] = jnp.zeros_like(table_pad)
    tokens_in.wait()
    table_in.wait()
    for head_id in range(head_count):
        table_pad[0:level_count, 0:table_count] = tab_ref[:, head_id, :]
        table_rows.append(table_pad[...] * scale)
    table_all = jnp.concatenate(table_rows, axis=0)
    high = table_all.astype(jnp.bfloat16)
    rest = table_all - high.astype(jnp.float32)
    middle = rest.astype(jnp.bfloat16)
    low = (rest - middle.astype(jnp.float32)).astype(jnp.bfloat16)
    split = jnp.concatenate([high, middle, low], axis=0)
    rows = head_count * padded

    def weigh(block):
        tokens = jnp.concatenate(
            [tok_ref[pl.ds(2 * block, 1), :], tok_ref[pl.ds(2 * block + 1, 1), :]], axis=1
        )
        picks = lax.broadcasted_iota(jnp.int32, (WIDTH, BLOCK), 0) == tokens
        one_hot = jnp.where(picks, 1.0, 0.0).astype(jnp.bfloat16)
        parts = jnp.dot(split, one_hot, preferred_element_type=jnp.float32)
        whole = parts[0:rows] + parts[rows : 2 * rows] + parts[2 * rows :]
        for head_id in range(head_count):
            weights[block, head_id] = whole[head_id * padded : (head_id + 1) * padded]

    def remote_copy(source, bit, head_id):
        return pltpu.make_async_remote_copy(
            src_ref=source,
            dst_ref=landed.at[bit, head_id],
            send_sem=send_sem.at[bit, head_id],
            recv_sem=recv_sem.at[bit, head_id],
            device_id={"ctx": me + 1},
            device_id_type=pl.DeviceIdType.MESH,
        )

    def has_bit(bit):
        return lax.rem(lax.div(me, 2**bit), 2) == 1

    def ends_span(bit):
        return lax.rem(me, 2**bit) == 2**bit - 1

    def is_source(bit):
        return jnp.logical_and(ends_span(bit), jnp.logical_not(has_bit(bit)))

    def is_relay(bit):
        return jnp.logical_and(has_bit(bit), jnp.logical_not(ends_span(bit)))

    def states(head_id, carry):
        @pl.when(head_id + 2 < head_count)
        def _():
            for part in range(1):
                load(1, head_id + 2, part).start()
                load(0, head_id + 2, part).start()

        for part in range(1):
            load(2, head_id, part).start()

        def turn(block):
            if block == 0:
                load(1, head_id, 0).wait()
                load(0, head_id, 0).wait()
            span = pl.ds(block * BLOCK, BLOCK)
            value_t = jnp.transpose(v_v[head_id, span, :])
            vt_v[head_id, :, span] = value_t
            return value_t

        value_next = turn(0)
        for block in range(block_count):
            span = pl.ds(block * BLOCK, BLOCK)
            value_t = value_next
            if block + 1 < block_count:
                value_next = turn(block + 1)
            if block % head_count == head_count - 1:
                weigh(head_id * (block_count // head_count) + block // head_count)
            state = jnp.dot(value_t, k_v[head_id, span, :], preferred_element_type=jnp.float32)
            bit = 0
            while block >> bit & 1:
                state = left[bit] + state
                bit += 1
            if bit < local_bits:
                left[bit] = state
                nodes[head_id, node_index(block_count, bit, block >> (bit + 1))] = state.astype(
                    jnp.bfloat16
                )
            else:
                total[head_id] = state
        for bit in range(device_bits):

            @pl.when(jnp.logical_not(has_bit(bit)))
            def _(bit=bit):
                landed[bit, head_id] = jnp.zeros((WIDTH, WIDTH), jnp.float32)

        if shards > 1:

            @pl.when(jnp.logical_and(head_id == 0, me < shards - 1))
            def _():
                pl.semaphore_wait(barrier, 1)

            @pl.when(is_source(0))
            def _():
                remote_copy(total.at[head_id], 0, head_id).start()

        return carry

    lax.fori_loop(0, head_count, states, 0)

    def service(bit, head_id):
        @pl.when(jnp.logical_and(has_bit(bit), me < shards - 1))
        def _():
            remote_copy(total.at[head_id], bit, head_id).wait_recv()

        @pl.when(is_relay(bit))
        def _():
            remote_copy(landed.at[bit, head_id], bit, head_id).start()

        if bit + 1 < device_bits:

            @pl.when(jnp.logical_and(ends_span(bit + 1), me < shards - 1))
            def _():
                base = total[head_id] if bit == 0 else lift[bit - 1, head_id]
                lift[bit, head_id] = base + landed[bit, head_id]

            @pl.when(is_source(bit + 1))
            def _():
                remote_copy(lift.at[bit, head_id], bit + 1, head_id).start()

    segment = block_count // 2
    due = sorted(
        (3 * bit + head_id, bit, head_id)
        for bit in range(device_bits)
        for head_id in range(head_count)
    )

    def weight_row(block, head_id, level_id):
        return weights[block, head_id, level_id : level_id + 1, :]

    def inside(head_id, carry):
        for part in range(1):
            load(2, head_id, part).wait()

        def levels_of(block):
            return [bit for bit in range(local_bits) if block >> bit & 1]

        def weigh_pairs(block):
            span = pl.ds(block * BLOCK, BLOCK)
            bits = levels_of(block)
            query = q_v[head_id, span, :]
            stack = [k_v[head_id, span, :]] + [
                nodes[head_id, node_index(block_count, bit, block >> (bit + 1))] for bit in bits
            ]
            product = lax.dot_general(
                jnp.concatenate(stack, axis=0), query, NT, preferred_element_type=jnp.float32
            )
            level_rows = [
                weight_row(block, head_id, level_id) for level_id in range(block_bits + 1)
            ]
            first = pair_tile([jnp.broadcast_to(row[:, :HALF], (8, HALF)) for row in level_rows])
            second = pair_tile([jnp.broadcast_to(row[:, HALF:], (8, HALF)) for row in level_rows])
            top = jnp.concatenate(
                [
                    (product[:HALF, :HALF] * first).astype(jnp.bfloat16),
                    (product[:HALF, HALF:] * level_rows[block_bits][:, HALF:]).astype(jnp.bfloat16),
                ],
                axis=1,
            )
            bottom = jnp.concatenate(
                [
                    jnp.zeros((HALF, HALF), jnp.bfloat16),
                    (product[HALF:BLOCK, HALF:] * second).astype(jnp.bfloat16),
                ],
                axis=1,
            )
            distant = None
            for place, bit in enumerate(bits):
                begin = BLOCK + place * WIDTH
                term = product[begin : begin + WIDTH] * weight_row(
                    block, head_id, block_bits + 1 + bit
                )
                distant = term if distant is None else distant + term
            return jnp.concatenate([top, bottom], axis=0), distant

        def pass_on(half):
            for point, bit, which in due:
                if point % 2 == half and point < 2 * head_count:

                    @pl.when(head_id == point // 2)
                    def _(bit=bit, which=which):
                        service(bit, which)

        pass_on(0)
        pairs_next = weigh_pairs(0)
        for block in range(block_count):
            if block == segment:
                pass_on(1)
            weighted, distant = pairs_next
            if block + 1 < block_count:
                pairs_next = weigh_pairs(block + 1)
            result = jnp.dot(
                vt_v[head_id, :, pl.ds(block * BLOCK, BLOCK)],
                weighted,
                preferred_element_type=jnp.float32,
            )
            acc[head_id, block] = result if distant is None else result + distant
        return carry

    lax.fori_loop(0, head_count, inside, 0)
    for point, bit, head_id in due:
        if point >= 2 * head_count:
            service(bit, head_id)

    if shards > 1:

        @pl.when(me == shards - 1)
        def _():
            for bit in range(device_bits):
                for head_id in range(head_count):
                    remote_copy(total.at[head_id], bit, head_id).wait_recv()

    for bit in range(device_bits):
        for head_id in range(head_count):
            remote[head_id, bit * WIDTH : (bit + 1) * WIDTH, :] = landed[bit, head_id].astype(
                jnp.bfloat16
            )
    for bit in range(device_bits):

        @pl.when(jnp.logical_or(is_source(bit), is_relay(bit)))
        def _(bit=bit):
            for head_id in range(head_count):
                remote_copy(total.at[head_id], bit, head_id).wait_send()


def finish_kernel(sizes, acc, q_v, remote, weights, out_hbm, out_v, out_sem):
    head_count, block_count, level_count, table_count, shards, device_bits = sizes
    first_level = BLOCK.bit_length() + block_count.bit_length() - 1
    padded = round_up(level_count, 8)
    chunk = max(1, block_count // 4)

    def write(head_id, part):
        column = pl.multiple_of(head_id * WIDTH, WIDTH)
        lines = pl.ds(part * chunk * BLOCK, chunk * BLOCK)
        return pltpu.make_async_copy(
            out_v.at[head_id, lines, :],
            out_hbm.at[lines, pl.ds(column, WIDTH)],
            out_sem.at[head_id, part],
        )

    def finish(head_id, carry):
        def add_up(block):
            result = acc[head_id, block]
            if device_bits:
                product = lax.dot_general(
                    remote[head_id],
                    q_v[head_id, pl.ds(block * BLOCK, BLOCK), :],
                    NT,
                    preferred_element_type=jnp.float32,
                )
            for bit in range(device_bits):
                row = weights[block, head_id, first_level + bit : first_level + bit + 1, :]
                result = result + product[bit * WIDTH : (bit + 1) * WIDTH] * row
            return result.astype(jnp.bfloat16)

        result_next = add_up(0)
        for block in range(block_count):
            result = result_next
            if block + 1 < block_count:
                result_next = add_up(block + 1)
            out_v[head_id, pl.ds(block * BLOCK, BLOCK), :] = jnp.transpose(result)
            if block % chunk == chunk - 1:
                write(head_id, block // chunk).start()
        return carry

    lax.fori_loop(0, head_count, finish, 0)
    for head_id in range(head_count):
        for part in range(block_count // chunk):
            write(head_id, part).wait()


def body(queries, key_vectors, value_vectors, token_rows, weight_table):
    table_count, head_count, level_count = weight_table.shape
    token_count = queries.shape[0]
    block_count = token_count // BLOCK
    shards = lax.axis_size("ctx")
    device_bits = shards.bit_length() - 1
    padded = round_up(level_count, 8)
    slots = max(1, device_bits)
    sizes = (head_count, block_count, level_count, table_count, shards, device_bits)
    hbm = pl.BlockSpec(memory_space=pltpu.HBM)
    vmem = pl.BlockSpec(memory_space=pltpu.VMEM)
    wide = (head_count, token_count, WIDTH)
    state = (WIDTH, WIDTH)
    acc, q_v, remote, weights = pl.pallas_call(
        functools.partial(kernel, sizes),
        out_shape=[
            jax.ShapeDtypeStruct((head_count, block_count, WIDTH, BLOCK), jnp.float32),
            jax.ShapeDtypeStruct(wide, jnp.bfloat16),
            jax.ShapeDtypeStruct((head_count, slots * WIDTH, WIDTH), jnp.bfloat16),
            jax.ShapeDtypeStruct((block_count, head_count, padded, BLOCK), jnp.float32),
        ],
        in_specs=[hbm] * 5,
        out_specs=[vmem] * 4,
        scratch_shapes=[
            pltpu.VMEM(wide, jnp.bfloat16),
            pltpu.VMEM(wide, jnp.bfloat16),
            pltpu.VMEM((head_count, WIDTH, token_count), jnp.bfloat16),
            pltpu.VMEM((head_count, max(1, block_count - 1)) + state, jnp.bfloat16),
            pltpu.VMEM((max(1, block_count.bit_length() - 1),) + state, jnp.float32),
            pltpu.VMEM((head_count,) + state, jnp.float32),
            pltpu.VMEM((slots, head_count) + state, jnp.float32),
            pltpu.VMEM((slots, head_count) + state, jnp.float32),
            pltpu.VMEM((token_count // WIDTH, WIDTH), jnp.int32),
            pltpu.VMEM((level_count, head_count, table_count), jnp.float32),
            pltpu.VMEM((padded, WIDTH), jnp.float32),
            pltpu.SemaphoreType.DMA((3, head_count, 1)),
            pltpu.SemaphoreType.DMA((2,)),
            pltpu.SemaphoreType.DMA((slots, head_count)),
            pltpu.SemaphoreType.DMA((slots, head_count)),
        ],
        compiler_params=pltpu.CompilerParams(
            collective_id=0, has_side_effects=True, vmem_limit_bytes=32 * 1024 * 1024
        ),
        cost_estimate=pl.CostEstimate(
            flops=10 * token_count * head_count * WIDTH * BLOCK,
            bytes_accessed=6 * token_count * head_count * WIDTH,
            transcendentals=0,
        ),
    )(
        *[
            pltpu.with_memory_space_constraint(operand, pltpu.HBM)
            for operand in (
                queries,
                key_vectors,
                value_vectors,
                token_rows.reshape(token_count // WIDTH, WIDTH),
                weight_table.transpose(2, 1, 0),
            )
        ]
    )
    return pl.pallas_call(
        functools.partial(finish_kernel, sizes),
        out_shape=jax.ShapeDtypeStruct(queries.shape, jnp.bfloat16),
        in_specs=[vmem] * 4,
        out_specs=hbm,
        scratch_shapes=[
            pltpu.VMEM(wide, jnp.bfloat16),
            pltpu.SemaphoreType.DMA((head_count, 4)),
        ],
        compiler_params=pltpu.CompilerParams(vmem_limit_bytes=32 * 1024 * 1024),
        cost_estimate=pl.CostEstimate(
            flops=4 * token_count * head_count * WIDTH * WIDTH,
            bytes_accessed=2 * token_count * head_count * WIDTH,
            transcendentals=0,
        ),
    )(acc, q_v, remote, weights)


def solution(mesh):
    placed = (
        P(("groups", "ctx"), "head"),
        P(("groups", "ctx"), "head"),
        P(("groups", "ctx"), "head"),
        P(("groups", "ctx")),
        P(None, "head", None),
    )
    return jax.shard_map(
        body, mesh=mesh, in_specs=placed, out_specs=P(("groups", "ctx"), "head"), check_vma=False
    )
```
